32 devices in a mesh: cores: 4 (over y, x), strip: 8 (over z, core).
Axes of the slice: x: 2, y: 2, z: 4, core: 2. Of those that a mesh axis runs over, the one named last changes fastest.
Arguments:
- potentials: float32 [64, 256, 2048], P('cores', None, 'strip'), may hold values from -6 to 6
- pair_include: int32 [64, 64], replicated, may hold values 0 or 1
- labels: int32 [256, 2048], P('strip', 'cores'), may hold values from 0 to 127
- conduct_across: float32 [256, 2048], P('strip', 'cores'), may hold values from 0.1 to 10
- conduct_down: float32 [256, 2048], P('strip', 'cores'), may hold values from 0.1 to 10
Outputs:
- current_across: float32 [256, 2048], P('strip', 'cores')
- current_down: float32 [256, 2048], P('strip', 'cores')
The draws below stay inside these ranges and needn't reach their ends.
Inputs may be any that keep to these rules, and one draw needn't show every extreme that they name: `labels`: a value below 64 names the core area that holds the cell; larger values mark cells outside every core area. `pair_include`: only entries above the diagonal are read.
All inputs are finite; a program needn't handle non-finite values.
Results may differ from the reference program's by a relative error of at most 0.00056.
Values may be sent and summed in bfloat16 or wider, within the bound.
No kernel may reach another device: no remote copies, remote signals or barrier semaphores. Data moves between devices by JAX's collectives and lax.ppermute only.
A program may use at most 64 MiB of HBM per device.

```python
import math
import jax
import jax.numpy as jnp
from jax import lax

K = 64
ROWS_DEV = 32
HEIGHT = 256
WIDTH = 2048
N_STRIP = 8


def touch_ends(array, key, least, largest):
    longest = array.shape.index(max(array.shape))
    spots = []
    for shift in (0, 1):
        where = [jax.random.randint(jax.random.fold_in(key, axis), (), 0, length) for axis, length in enumerate(array.shape)]
        where[longest] = (where[longest] + shift) % array.shape[longest]
        spots.append(tuple(where))
    return array.at[spots[0]].set(least).at[spots[1]].set(largest)


def shard_levels(key, extent, cuts, least, top_value):
    factor_of = 1.0
    for dim, blocks in cuts:
        draws = jax.random.uniform(jax.random.fold_in(jax.random.fold_in(key, 6), dim), (blocks,), jnp.float32, least / len(cuts), top_value / len(cuts))
        factor_of = factor_of * jnp.repeat(jnp.exp(draws), extent[dim] // blocks).reshape((-1,) + (1,) * (len(extent) - 1 - dim))
    return factor_of


def gaussian(rng, extent, deviation, bound, pieces=(), held_as=jnp.bfloat16):
    gain = shard_levels(rng, extent, pieces, -0.22, 0.18) if pieces else 1.0
    entries = jax.random.normal(rng, extent, jnp.float32) * deviation * gain
    return jnp.minimum(jnp.maximum(entries, -bound), bound).astype(held_as)


def setup_inputs(seed: int = 0) -> dict:
    key_list = jax.random.split(jax.random.key(seed), 6)
    return {
        "potentials": gaussian(key_list[0], (K, HEIGHT, WIDTH), 1.0, 6.0, ((0, 4), (2, 8)), jnp.float32),
        "pair_include": touch_ends((jax.random.randint(key_list[1], (K, K), 0, 4) < 3).astype(jnp.int32), jax.random.fold_in(key_list[1], 1), 0, 1),
        "labels": touch_ends(jax.random.randint(key_list[2], (HEIGHT, WIDTH), 0, 2 * K), jax.random.fold_in(key_list[2], 1), 0, (2 * K) - 1).astype(jnp.int32),
        "conduct_across": jnp.clip(jnp.exp(math.log(10.0) - 4.6051702 * jax.random.uniform(key_list[3], (HEIGHT, WIDTH), jnp.float32) ** shard_levels(key_list[3], (HEIGHT, WIDTH), ((0, 8), (1, 4)), -0.2, 0.2)), 0.1, 10.0),
        "conduct_down": jnp.clip(jnp.exp(math.log(10.0) - 4.6051702 * jax.random.uniform(key_list[4], (HEIGHT, WIDTH), jnp.float32) ** shard_levels(key_list[4], (HEIGHT, WIDTH), ((0, 8), (1, 4)), -0.2, 0.2)), 0.1, 10.0),
    }


def reference(potentials, pair_include, labels, conduct_across, conduct_down):
    field_count, height, width = potentials.shape
    sideways = jnp.concatenate([potentials[:, :, 1:] - potentials[:, :, :-1], jnp.zeros((field_count, height, 1), jnp.float32)], axis=2).astype(jnp.bfloat16)
    downward = jnp.concatenate([potentials[:, 1:, :] - potentials[:, :-1, :], jnp.zeros((field_count, 1, width), jnp.float32)], axis=1).astype(jnp.bfloat16)
    field_ids = jnp.arange(field_count, dtype=jnp.int32)
    weights = jnp.where(field_ids[None, :] > field_ids[:, None], pair_include.astype(jnp.float32), jnp.float32(0.0))

    def band_sums(inputs):
        band_across, band_down, band_labels = inputs
        cell_count = ROWS_DEV * width
        flat_across = band_across.reshape(field_count, cell_count).astype(jnp.float32)
        flat_down = band_down.reshape(field_count, cell_count).astype(jnp.float32)
        labels_flat = band_labels.reshape(cell_count)
        other_keep = labels_flat[None, :] != field_ids[:, None]

        def accumulate(number, totals):
            own_across = lax.dynamic_index_in_dim(flat_across, number, 0, keepdims=False)
            own_down = lax.dynamic_index_in_dim(flat_down, number, 0, keepdims=False)
            weight_row = lax.dynamic_index_in_dim(weights, number, 0, keepdims=False)
            factor = jnp.where(other_keep, weight_row[:, None], jnp.float32(0.0))
            term_across = jnp.sum(factor * jnp.abs(own_across[None, :] - flat_across), axis=0)
            term_down = jnp.sum(factor * jnp.abs(own_down[None, :] - flat_down), axis=0)
            keep_own = labels_flat != number
            return (totals[0] + jnp.where(keep_own, term_across, jnp.float32(0.0)),
                    totals[1] + jnp.where(keep_own, term_down, jnp.float32(0.0)))

        empty_sum = jnp.zeros((cell_count,), jnp.float32)
        return lax.fori_loop(0, field_count, accumulate, (empty_sum, empty_sum))

    bands_across = sideways.reshape(field_count, N_STRIP, ROWS_DEV, width).transpose(1, 0, 2, 3)
    bands_down = downward.reshape(field_count, N_STRIP, ROWS_DEV, width).transpose(1, 0, 2, 3)
    labels_bands = labels.reshape(N_STRIP, ROWS_DEV, width)
    total_across, total_down = lax.map(band_sums, (bands_across, bands_down, labels_bands))
    scale = 2.0 / (field_count * (field_count - 1))
    return (conduct_across * (total_across.reshape(height, width) * scale),
            conduct_down * (total_down.reshape(height, width) * scale))
```

```python
import functools

import jax
import jax.numpy as jnp
from jax import lax
from jax.experimental import pallas as pl
from jax.experimental.pallas import tpu as pltpu
from jax.sharding import PartitionSpec as P

PARTNERS = 4
LOW = -64.0
LANES = 128
VMEM = pl.BlockSpec(memory_space=pltpu.VMEM)
SMEM = pl.BlockSpec(memory_space=pltpu.SMEM)
LIMIT = pltpu.CompilerParams(vmem_limit_bytes=32 * 2**20)


def prepare_kernel(include_ref, groups_ref, linear_ref):
    fields = include_ref.shape[0]
    slots = groups_ref.shape[1]
    f32 = jnp.float32

    def dot(a, b, over):
        return lax.dot_general(
            a.astype(jnp.bfloat16),
            b.astype(jnp.bfloat16),
            ((over[:1], over[1:]), ((), ())),
            preferred_element_type=f32,
        )

    row = lax.broadcasted_iota(jnp.int32, (fields, fields), 0)
    column = lax.broadcasted_iota(jnp.int32, (fields, fields), 1)
    upper = jnp.where(column > row, 1.0, 0.0)
    lower = jnp.where(column < row, 1.0, 0.0)
    eye = jnp.where(column == row, 1.0, 0.0)
    included = jnp.where(column > row, include_ref[...], 0).astype(f32)
    place = dot(included, upper, (1, 0))
    both = included + dot(included, eye, (0, 0))
    count = jnp.sum(included, axis=1, keepdims=True)
    degree = jnp.sum(both, axis=1, keepdims=True)
    groups = jnp.floor((count + (PARTNERS - 1)) * (1.0 / PARTNERS))
    start = dot(lower, jnp.broadcast_to(groups, (fields, LANES)), (1, 0))[:, :1]
    total = jnp.sum(groups, axis=0, keepdims=True)
    slot = lax.broadcasted_iota(jnp.int32, (fields, slots), 1).astype(f32)
    ids = lax.broadcasted_iota(jnp.int32, (fields, slots), 0).astype(f32)
    inside = jnp.where((slot >= start) & (slot < start + groups), 1.0, 0.0)
    used = jnp.sum(inside, axis=0, keepdims=True)
    own = jnp.sum(inside * ids, axis=0, keepdims=True)
    first = jnp.sum(inside * (slot - start) * PARTNERS, axis=0, keepdims=True)
    places = dot(jnp.where(included > 0, place, -8.0), inside, (0, 0))
    places = jnp.where(used > 0, places, -8.0)
    groups_ref[...] = jnp.zeros(groups_ref.shape, jnp.int32)
    for u in range(PARTNERS):
        hit = jnp.where(places == first + u, 1.0, 0.0)
        found = jnp.sum(hit, axis=0, keepdims=True)
        partner = jnp.sum(hit * ids, axis=0, keepdims=True)
        absent = jnp.where(used > 0, float(fields), float(fields + 1))
        groups_ref[u : u + 1, :] = jnp.where(found > 0, partner, absent).astype(jnp.int32)
    owner = jnp.where(used > 0, own, float(fields + 1))
    groups_ref[PARTNERS : PARTNERS + 1, :] = owner.astype(jnp.int32)
    groups_ref[PARTNERS + 1 : PARTNERS + 2, :] = jnp.broadcast_to(total, (1, slots)).astype(
        jnp.int32
    )
    lanes = linear_ref.shape[1]
    padding = 2.0 * (groups * PARTNERS - count)
    wide = jnp.concatenate([both, jnp.zeros((fields, lanes - fields), f32)], axis=1)
    row = lax.broadcasted_iota(jnp.int32, (fields, lanes), 0)
    column = lax.broadcasted_iota(jnp.int32, (fields, lanes), 1)
    linear_ref[...] = jnp.where(row == column, 0.0, degree + wide) + padding


def prepare(pair_include):
    fields = pair_include.shape[0]
    most = sum(pl.cdiv(fields - 1 - a, PARTNERS) for a in range(fields))
    slots = pl.cdiv(most + 8, LANES) * LANES
    groups, linear = pl.pallas_call(
        prepare_kernel,
        out_shape=(
            jax.ShapeDtypeStruct((8, slots), jnp.int32),
            jax.ShapeDtypeStruct((fields, LANES), jnp.float32),
        ),
        compiler_params=LIMIT,
        name="prepare",
    )(pair_include)
    return groups.T.reshape(-1), linear


def pairs_kernel(base_ref, groups_ref, *refs, scale, unroll):
    *parts, labels_ref, linear_ref, out_ref, held = refs
    fields = linear_ref.shape[0]
    each = parts[0].shape[0]
    rows, width = out_ref.shape
    labels = labels_ref[...]
    held[fields] = jnp.full((rows, width), LOW, jnp.float32)
    held[fields + 1] = jnp.zeros((rows, width), jnp.float32)
    linear = jnp.zeros((rows, width), jnp.float32)
    for k, part in enumerate(parts):
        for i in range(each):
            field = base_ref[k] + i
            values = jnp.where(labels == field, LOW, part[i].astype(jnp.float32))
            held[field] = values
            table = jnp.broadcast_to(linear_ref[pl.ds(field, 1), :], (rows, LANES))
            factor = jnp.concatenate(
                [
                    jnp.take_along_axis(table, labels[:, at : at + LANES], axis=1)
                    for at in range(0, width, LANES)
                ],
                axis=1,
            )
            linear = linear + factor * values

    def step(number, total):
        for v in range(unroll):
            at = (number * unroll + v) * 8
            own = held[groups_ref[at + PARTNERS]]
            for u in range(PARTNERS):
                total = total + jnp.maximum(own, held[groups_ref[at + u]])
        return total

    steps = (groups_ref[PARTNERS + 1] + (unroll - 1)) // unroll
    total = lax.fori_loop(0, steps, step, jnp.zeros((rows, width), jnp.float32))
    out_ref[...] = (2.0 * total - linear) * scale


def pairs(base, groups, parts, labels, linear):
    fields = linear.shape[0]
    work = fields * fields * labels.size
    return pl.pallas_call(
        functools.partial(pairs_kernel, scale=2.0 / (fields * (fields - 1)), unroll=8),
        in_specs=[SMEM, SMEM] + [VMEM] * (len(parts) + 2),
        out_specs=VMEM,
        out_shape=jax.ShapeDtypeStruct(labels.shape, jnp.float32),
        scratch_shapes=[pltpu.VMEM((fields + 2, *labels.shape), jnp.float32)],
        compiler_params=LIMIT,
        cost_estimate=pl.CostEstimate(flops=work, bytes_accessed=work // 16, transcendentals=0),
        name="pairs",
    )(base, groups, *parts, labels, linear)


def down_kernel(spots_ref, *refs, count, last):
    mains, nexts, outs = refs[:count], refs[count : 2 * count], refs[2 * count :]
    for k in range(count):
        each, rows, width = outs[k].shape
        at_end = spots_ref[k] == last
        row = lax.broadcasted_iota(jnp.int32, (rows, width), 0)
        for i in range(each):
            here = mains[k][i]
            below = jnp.concatenate([here[1:], nexts[k][i, 0:1, :]], axis=0)
            change = jnp.where((row == rows - 1) & at_end, 0.0, below - here)
            outs[k][i] = change.astype(jnp.bfloat16)


def side_kernel(spots_ref, *refs, count):
    mains, besides, outs = refs[:count], refs[count : 2 * count], refs[2 * count :]
    at_end = spots_ref[count] == 1
    for k in range(count):
        each, rows, width = outs[k].shape
        lane = lax.broadcasted_iota(jnp.int32, (rows, width), 1)
        for i in range(each):
            here = mains[k][i]
            right = jnp.where(
                lane == width - 1, besides[k][:, i : i + 1], pltpu.roll(here, width - 1, 1)
            )
            change = jnp.where((lane == width - 1) & at_end, 0.0, right - here)
            outs[k][i] = change.astype(jnp.bfloat16)


def differences(kind, potentials, beside, spots, last_strip, rows):
    each, height, width = potentials.shape
    count = spots.shape[0]

    def main_spec(k):
        return pl.BlockSpec((each, rows, width), lambda i, at: (0, at[k], 0))

    if kind == "down":

        def next_spec(k):
            return pl.BlockSpec(
                (each, 8, width),
                lambda i, at: (0, jnp.minimum((at[k] + 1) * (rows // 8), height // 8 - 1), 0),
            )

        other, specs = potentials, [next_spec(k) for k in range(count)]
        body = functools.partial(down_kernel, count=count, last=height // rows - 1)
    else:

        def beside_spec(k):
            return pl.BlockSpec((rows, LANES), lambda i, at: (at[k], 0))

        other, specs = beside, [beside_spec(k) for k in range(count)]
        body = functools.partial(side_kernel, count=count)
    scalars = jnp.concatenate([spots, last_strip.astype(jnp.int32)[None]])
    return pl.pallas_call(
        body,
        grid_spec=pltpu.PrefetchScalarGridSpec(
            num_scalar_prefetch=1,
            grid=(1,),
            in_specs=[main_spec(k) for k in range(count)] + specs,
            out_specs=[pl.BlockSpec((each, rows, width), lambda i, at: (0, 0, 0))] * count,
        ),
        out_shape=[jax.ShapeDtypeStruct((each, rows, width), jnp.bfloat16)] * count,
        compiler_params=LIMIT,
        cost_estimate=pl.CostEstimate(
            flops=4 * count * each * rows * width,
            bytes_accessed=6 * count * each * rows * width,
            transcendentals=0,
        ),
        name=kind,
    )(scalars, *([potentials] * count), *([other] * count))


def edge_kernel(potentials_ref, out_ref):
    each, rows, _ = potentials_ref.shape
    lane = lax.broadcasted_iota(jnp.int32, (rows, LANES), 1)
    edge = jnp.zeros((rows, LANES), jnp.float32)
    for i in range(each):
        edge = jnp.where(lane == i, potentials_ref[i][:, 0:1], edge)
    out_ref[...] = edge


def first_columns(potentials):
    each, height, _ = potentials.shape
    rows = 64
    return pl.pallas_call(
        edge_kernel,
        grid=(height // rows,),
        in_specs=[pl.BlockSpec((each, rows, LANES), lambda i: (0, i, 0))],
        out_specs=pl.BlockSpec((rows, LANES), lambda i: (i, 0)),
        out_shape=jax.ShapeDtypeStruct((height, LANES), jnp.float32),
        compiler_params=LIMIT,
        name="edge",
    )(potentials)


def finish_kernel(halves_ref, *refs, chunks, width):
    pieces, (across, down, out_across, out_down) = refs[: len(chunks)], refs[len(chunks) :]
    for (kind, turn, first, rows), piece in zip(chunks, pieces):
        conduct, out = (down, out_down) if kind == "down" else (across, out_across)
        lanes = pl.ds(pl.multiple_of(halves_ref[turn] * width, width), width)
        out[first : first + rows, lanes] = conduct[first : first + rows, lanes] * piece[...]


def finish(chunks, halves, pieces, conduct_across, conduct_down):
    shape = jax.ShapeDtypeStruct(conduct_across.shape, jnp.float32)
    return pl.pallas_call(
        functools.partial(finish_kernel, chunks=chunks, width=pieces[0].shape[1]),
        in_specs=[SMEM] + [VMEM] * (len(pieces) + 2),
        out_specs=[VMEM, VMEM],
        out_shape=[shape, shape],
        compiler_params=LIMIT,
        name="finish",
    )(halves, *pieces, conduct_across, conduct_down)


def local(potentials, pair_include, labels, conduct_across, conduct_down):
    groups_of, strips = lax.axis_size("cores"), lax.axis_size("strip")
    core, strip = lax.axis_index("cores"), lax.axis_index("strip")
    each, height, width = potentials.shape
    band_rows = labels.shape[0]
    turns = strips // groups_of
    paired = groups_of & (groups_of - 1) == 0

    def towards(index, k):
        return index ^ k if paired else (index + k) % groups_of

    def source(index, k):
        return index ^ k if paired else (index + groups_of - k) % groups_of

    def moves(turn, home):
        out = []
        for c in range(groups_of):
            for s in range(strips):
                band = c * turns + (s + turn) % turns
                here, there = c * strips + s, (s // turns) * strips + band
                out.append((here, there) if home else (there, here))
        return out

    chunks = [
        (kind, turn, 0, band_rows) for kind in ("down", "side") for turn in range(turns)
    ]
    base = jnp.stack([source(core, k) * each for k in range(groups_of)]).astype(jnp.int32)
    halves = jnp.stack([(strip + turns - t % turns) % turns for t in range(turns)]).astype(
        jnp.int32
    )
    last_strip = strip == strips - 1

    def spots(turn, first, rows):
        band = [towards(core, k) * turns + (strip + turn) % turns for k in range(groups_of)]
        return (jnp.stack(band) * (band_rows // rows) + first // rows).astype(jnp.int32)

    def exchange(kind, turn, first, rows, beside):
        blocks = differences(
            kind, potentials, beside, spots(turn, first, rows), last_strip, rows
        )
        return [blocks[0]] + [
            lax.ppermute(
                blocks[k], "cores", [(i, towards(i, k)) for i in range(groups_of)]
            )
            for k in range(1, groups_of)
        ]

    beside = lax.ppermute(
        first_columns(potentials), "strip", [(i, i - 1) for i in range(1, strips)]
    )
    own_labels = []
    for turn in range(turns):
        half = lax.dynamic_slice_in_dim(labels, halves[turn] * width, width, 1)
        own_labels.append(lax.ppermute(half, ("cores", "strip"), moves(turn, False)))
    groups, linear = prepare(pair_include)
    pieces = []
    for kind, turn, first, rows in chunks:
        parts = exchange(kind, turn, first, rows, beside)
        sums = pairs(
            base, groups, parts, own_labels[turn][first : first + rows], linear
        )
        pieces.append(lax.ppermute(sums, ("cores", "strip"), moves(turn, True)))
    return finish(chunks, halves, pieces, conduct_across, conduct_down)


def solution(mesh):
    return jax.shard_map(
        local,
        mesh=mesh,
        in_specs=(
            P("cores", None, "strip"),
            P(),
            P("strip", "cores"),
            P("strip", "cores"),
            P("strip", "cores"),
        ),
        out_specs=(P("strip", "cores"), P("strip", "cores")),
        check_vma=False,
    )
```

```python
import functools

import jax
import jax.numpy as jnp
from jax import lax
from jax.experimental import pallas as pl
from jax.experimental.pallas import tpu as pltpu
from jax.sharding import PartitionSpec as P

PARTNERS = 4
LOW = -64.0
LANES = 128
VMEM = pl.BlockSpec(memory_space=pltpu.VMEM)
SMEM = pl.BlockSpec(memory_space=pltpu.SMEM)
HBM = pl.BlockSpec(memory_space=pltpu.HBM)
LOADS = 4
LIMIT = pltpu.CompilerParams(vmem_limit_bytes=16 * 2**20)
ALL = pltpu.CompilerParams(vmem_limit_bytes=60 * 2**20)


def prepare_kernel(include_ref, groups_ref, linear_ref):
    fields = include_ref.shape[0]
    slots = groups_ref.shape[1]
    f32 = jnp.float32

    def dot(a, b, over):
        return lax.dot_general(
            a.astype(jnp.bfloat16),
            b.astype(jnp.bfloat16),
            ((over[:1], over[1:]), ((), ())),
            preferred_element_type=f32,
        )

    row = lax.broadcasted_iota(jnp.int32, (fields, fields), 0)
    column = lax.broadcasted_iota(jnp.int32, (fields, fields), 1)
    upper = jnp.where(column > row, 1.0, 0.0)
    lower = jnp.where(column < row, 1.0, 0.0)
    eye = jnp.where(column == row, 1.0, 0.0)
    included = jnp.where(column > row, include_ref[...], 0).astype(f32)
    place = dot(included, upper, (1, 0))
    both = included + dot(included, eye, (0, 0))
    count = jnp.sum(included, axis=1, keepdims=True)
    degree = jnp.sum(both, axis=1, keepdims=True)
    groups = jnp.floor((count + (PARTNERS - 1)) * (1.0 / PARTNERS))
    start = dot(lower, jnp.broadcast_to(groups, (fields, LANES)), (1, 0))[:, :1]
    total = jnp.sum(groups, axis=0, keepdims=True)
    slot = lax.broadcasted_iota(jnp.int32, (fields, slots), 1).astype(f32)
    ids = lax.broadcasted_iota(jnp.int32, (fields, slots), 0).astype(f32)
    inside = jnp.where((slot >= start) & (slot < start + groups), 1.0, 0.0)
    used = jnp.sum(inside, axis=0, keepdims=True)
    own = jnp.sum(inside * ids, axis=0, keepdims=True)
    first = jnp.sum(inside * (slot - start) * PARTNERS, axis=0, keepdims=True)
    places = dot(jnp.where(included > 0, place, -8.0), inside, (0, 0))
    places = jnp.where(used > 0, places, -8.0)
    groups_ref[...] = jnp.zeros(groups_ref.shape, jnp.int32)
    for u in range(PARTNERS):
        hit = jnp.where(places == first + u, 1.0, 0.0)
        found = jnp.sum(hit, axis=0, keepdims=True)
        partner = jnp.sum(hit * ids, axis=0, keepdims=True)
        absent = jnp.where(used > 0, float(fields), float(fields + 1))
        groups_ref[u : u + 1, :] = jnp.where(found > 0, partner, absent).astype(jnp.int32)
    owner = jnp.where(used > 0, own, float(fields + 1))
    groups_ref[PARTNERS : PARTNERS + 1, :] = owner.astype(jnp.int32)
    groups_ref[PARTNERS + 1 : PARTNERS + 2, :] = jnp.broadcast_to(total, (1, slots)).astype(
        jnp.int32
    )
    lanes = linear_ref.shape[1]
    padding = 2.0 * (groups * PARTNERS - count)
    wide = jnp.concatenate([both, jnp.zeros((fields, lanes - fields), f32)], axis=1)
    row = lax.broadcasted_iota(jnp.int32, (fields, lanes), 0)
    column = lax.broadcasted_iota(jnp.int32, (fields, lanes), 1)
    linear_ref[...] = jnp.where(row == column, 0.0, degree + wide) + padding


def prepare(pair_include):
    fields = pair_include.shape[0]
    most = sum(pl.cdiv(fields - 1 - a, PARTNERS) for a in range(fields))
    slots = pl.cdiv(most + 8, LANES) * LANES
    groups, linear = pl.pallas_call(
        prepare_kernel,
        out_shape=(
            jax.ShapeDtypeStruct((8, slots), jnp.int32),
            jax.ShapeDtypeStruct((fields, LANES), jnp.float32),
        ),
        compiler_params=LIMIT,
        name="prepare",
    )(pair_include)
    return groups.T.reshape(-1), linear


def factors_kernel(labels_ref, linear_ref, out_ref):
    turns, fields, band, width = out_ref.shape

    def one(field, carry):
        table = jnp.broadcast_to(linear_ref[pl.ds(field, 1), :], (band, LANES))
        for t in range(turns):
            mine = labels_ref[t * band : (t + 1) * band, :]
            factor = jnp.concatenate(
                [
                    jnp.take_along_axis(table, mine[:, at : at + LANES], axis=1)
                    for at in range(0, width, LANES)
                ],
                axis=1,
            )
            out_ref[t, field] = factor.astype(jnp.bfloat16)
        return carry

    lax.fori_loop(0, fields, one, 0, unroll=4)


def pairs_kernel(base_ref, groups_ref, *refs, scale, unroll, at_turn, label_turn):
    *parts, labels_ref, factors_ref, out_ref, held = refs
    fields = factors_ref.shape[1]
    _, each, rows, width = parts[0].shape
    held[fields] = jnp.full((rows, width), LOW, jnp.float32)
    held[fields + 1] = jnp.zeros((rows, width), jnp.float32)
    labels = labels_ref[...]
    linear = jnp.zeros((rows, width), jnp.float32)
    for k, part in enumerate(parts):
        for i in range(each):
            field = base_ref[k] + i
            values = jnp.where(labels == field, LOW, part[at_turn, i].astype(jnp.float32))
            held[field] = values
            linear = linear + factors_ref[label_turn, field].astype(jnp.float32) * values

    def step(number, total):
        for v in range(unroll):
            at = (number * unroll + v) * 8
            own = held[groups_ref[at + PARTNERS]]
            for u in range(PARTNERS):
                total = total + jnp.maximum(own, held[groups_ref[at + u]])
        return total

    steps = (groups_ref[PARTNERS + 1] + (unroll - 1)) // unroll
    total = lax.fori_loop(0, steps, step, jnp.zeros((rows, width), jnp.float32))
    out_ref[...] = (2.0 * total - linear) * scale


def pairs(base, groups, parts, labels, factors, at_turn, label_turn):
    fields = factors.shape[1]
    work = fields * fields * labels.size
    return pl.pallas_call(
        functools.partial(
            pairs_kernel,
            scale=2.0 / (fields * (fields - 1)),
            unroll=8,
            at_turn=at_turn,
            label_turn=label_turn,
        ),
        in_specs=[SMEM, SMEM] + [VMEM] * (len(parts) + 2),
        out_specs=VMEM,
        out_shape=jax.ShapeDtypeStruct(labels.shape, jnp.float32),
        scratch_shapes=[pltpu.VMEM((fields + 2, *labels.shape), jnp.float32)],
        compiler_params=LIMIT,
        cost_estimate=pl.CostEstimate(flops=work, bytes_accessed=work // 16, transcendentals=0),
        name="pairs",
    )(base, groups, *parts, labels, factors)


def load_fields(potentials_ref, held, sems):
    each = held.shape[0]
    step = max(each // LOADS, 1)
    copies = []
    for number, at in enumerate(range(0, each, step)):
        span = pl.ds(at, step)
        copies.append(
            pltpu.make_async_copy(potentials_ref.at[span], held.at[span], sems.at[number])
        )
        copies[-1].start()
    for number, copy in enumerate(copies):
        copy.wait()
        yield from range(number * step, (number + 1) * step)


def down_kernel(first_ref, potentials_ref, *refs):
    *outs, edge_ref, held, sems = refs
    _, height, width = held.shape
    turns, _, rows, _ = outs[0].shape
    row = lax.broadcasted_iota(jnp.int32, (rows, width), 0)
    lane = lax.broadcasted_iota(jnp.int32, (height, LANES), 1)
    for i in load_fields(potentials_ref, held, sems):
        for k, out in enumerate(outs):
            for t in range(turns):
                first = pl.multiple_of(first_ref[k * turns + t] * rows, rows)
                following = pl.multiple_of(jnp.minimum(first + rows, height - 8), 8)
                at_end = first + rows == height
                here = held[i, pl.ds(first, rows), :]
                below = held[i, pl.ds(following, 8), :]
                below = jnp.concatenate([here[1:], below[:1]], axis=0)
                change = jnp.where((row == rows - 1) & at_end, 0.0, below - here)
                out[t, i] = change.astype(jnp.bfloat16)
        edge_ref[...] = jnp.where(lane == i, held[i, :, 0:1], edge_ref[...] if i else 0.0)


def side_kernel(first_ref, potentials_ref, beside_ref, *outs, turns):
    _, each, rows, width = outs[0].shape
    parts = len(outs) // turns
    lane = lax.broadcasted_iota(jnp.int32, (rows, width), 1)
    at_end = first_ref[len(outs)] == 1
    for k in range(parts):
        for t in range(turns):
            first = pl.multiple_of(first_ref[k * turns + t] * rows, rows)
            for i in range(each):
                here = potentials_ref[i, pl.ds(first, rows), :]
                right = pltpu.roll(here, width - 1, 1)
                beside = beside_ref[pl.ds(first, rows), i : i + 1]
                right = jnp.where(lane == width - 1, beside, right)
                change = jnp.where((lane == width - 1) & at_end, 0.0, right - here)
                outs[t * parts + k][0, i] = change.astype(jnp.bfloat16)


def on_tile(body, name, out_shape, scalars, *arrays, fields=None):
    work = sum(a.size for a in arrays)
    specs = [VMEM] * len(arrays)
    scratch = []
    if fields is not None:
        arrays, specs = (fields, *arrays), [HBM, *specs]
        scratch = [pltpu.VMEM(fields.shape, fields.dtype), pltpu.SemaphoreType.DMA((LOADS,))]
        work = 2 * fields.size
    return pl.pallas_call(
        body,
        in_specs=[SMEM] * len(scalars) + specs,
        out_specs=jax.tree.map(lambda _: VMEM, out_shape),
        out_shape=out_shape,
        scratch_shapes=scratch,
        compiler_params=LIMIT if fields is None else ALL,
        cost_estimate=pl.CostEstimate(
            flops=4 * work, bytes_accessed=6 * work, transcendentals=0
        ),
        name=name,
    )(*scalars, *arrays)


def finish_kernel(halves_ref, *refs, chunks, width):
    *pieces, across, down, out_across, out_down = refs
    for (turn, contents), piece in zip(chunks, pieces):
        lanes = pl.ds(pl.multiple_of(halves_ref[turn] * width, width), width)
        at = 0
        for kind, first, rows in contents:
            conduct, out = (down, out_down) if kind == "down" else (across, out_across)
            out[first : first + rows, lanes] = (
                conduct[first : first + rows, lanes] * piece[at : at + rows]
            )
            at += rows


def finish(chunks, halves, pieces, conduct_across, conduct_down):
    shape = jax.ShapeDtypeStruct(conduct_across.shape, jnp.float32)
    return pl.pallas_call(
        functools.partial(finish_kernel, chunks=chunks, width=pieces[0].shape[1]),
        in_specs=[SMEM] + [VMEM] * (len(pieces) + 2),
        out_specs=[VMEM, VMEM],
        out_shape=[shape, shape],
        compiler_params=LIMIT,
        name="finish",
    )(halves, *pieces, conduct_across, conduct_down)


def after(value, *others):
    return lax.optimization_barrier((value, *others))[0]


def towards(index, step, size):
    return index ^ step if size & (size - 1) == 0 else (index + step) % size


def source(index, step, size):
    return index ^ step if size & (size - 1) == 0 else (index + size - step) % size


def local(potentials, pair_include, labels, conduct_across, conduct_down):
    parts, strips = lax.axis_size("cores"), lax.axis_size("strip")
    core, strip = lax.axis_index("cores"), lax.axis_index("strip")
    each, height, width = potentials.shape
    rows = labels.shape[0]
    turns = strips // parts

    flat = [(c, s // turns, s % turns) for c in range(parts) for s in range(strips)]

    def number(c, group, j):
        return c * strips + group * turns + j

    def move(array, to):
        moves = [(number(*at), number(*to(*at))) for at in flat]
        return lax.ppermute(array, ("cores", "strip"), moves)

    def send_home(array, turn):
        return move(array, lambda c, g, j: (g, c, towards(j, turn, turns)))

    def exchange(block, k):
        moves = [(i, towards(i, k, parts)) for i in range(parts)]
        return lax.ppermute(block, "cores", moves)

    inside = strip % turns
    ts = jnp.arange(turns, dtype=jnp.int32)
    ks = jnp.arange(parts, dtype=jnp.int32)
    base = source(core, ks, parts) * each
    first = towards(core, ks, parts)[:, None] * turns + towards(inside, ts, turns)[None]
    last = (strip == strips - 1).astype(jnp.int32)
    first = jnp.concatenate([first.reshape(-1), last[None]])
    halves = source(inside, ts, turns)

    block = jax.ShapeDtypeStruct((turns, each, rows, width), jnp.bfloat16)
    column = jax.ShapeDtypeStruct((height, LANES), jnp.float32)
    *down, edge = on_tile(
        down_kernel, "down", [block] * parts + [column], [first], fields=potentials
    )
    far = list(range(parts - 1, 0, -1))
    down = [down[0], *[exchange(down[k], k) for k in far][::-1]]
    beside = lax.ppermute(edge, "strip", [(i, i - 1) for i in range(1, strips)])
    labels = move(after(labels, edge), lambda c, g, j: (g, c, j))
    groups, linear = prepare(after(pair_include, edge))

    own_labels = []
    for t in range(turns):
        to = towards(inside, t, turns)
        part = lax.dynamic_slice_in_dim(labels, to * width, width, 1)
        back = (turns - t) % turns if turns & (turns - 1) else t
        own_labels.append((back, move(part, lambda c, g, j: (c, g, towards(j, t, turns))) if t else part))
    own_labels = [part for _, part in sorted(own_labels, key=lambda pair: pair[0])]

    block = jax.ShapeDtypeStruct((1, each, rows, width), jnp.bfloat16)
    side = on_tile(
        functools.partial(side_kernel, turns=turns),
        "side",
        [block] * (parts * turns),
        [after(first, *own_labels, groups)],
        potentials,
        beside,
    )
    factors = on_tile(
        factors_kernel,
        "factors",
        jax.ShapeDtypeStruct((turns, parts * each, rows, width), jnp.bfloat16),
        [],
        jnp.concatenate(own_labels, axis=0),
        after(linear, *side),
    )
    blocks = [side[t * parts : (t + 1) * parts] for t in range(turns)]
    down[0] = after(down[0], *down[1:])
    down_sums = [pairs(base, groups, down, own_labels[t], factors, t, t) for t in range(turns)]
    arrived = []
    for t in range(turns):
        got = [blocks[t][0]]
        for k in far:
            if t == 0:
                waits = [factors] if k == 1 else []
            else:
                waits = [down_sums[min(t, turns - 1) if k == 1 else t - 1]]
            got.insert(1, exchange(after(blocks[t][k], *waits), k))
        arrived.append(got)
    side_sums, pieces = [], []
    for t in range(turns):
        got = arrived[t]
        got[0] = after(got[0], (side_sums or down_sums)[-1])
        side_sums.append(pairs(base, groups, got, own_labels[t], factors, 0, t))
        joined = jnp.concatenate([down_sums[t], side_sums[t]], axis=0)
        pieces.append(send_home(joined, t))
    contents = tuple((t, (("down", 0, rows), ("side", 0, rows))) for t in range(turns))
    return finish(contents, halves, pieces, conduct_across, conduct_down)


def solution(mesh):
    return jax.shard_map(
        local,
        mesh=mesh,
        in_specs=(
            P("cores", None, "strip"),
            P(),
            P("strip", "cores"),
            P("strip", "cores"),
            P("strip", "cores"),
        ),
        out_specs=(P("strip", "cores"), P("strip", "cores")),
        check_vma=False,
    )
```

```python
import functools

import jax
import jax.numpy as jnp
from jax import lax
from jax.experimental import pallas as pl
from jax.experimental.pallas import tpu as pltpu
from jax.sharding import PartitionSpec as P

PARTNERS = 4
LOW = -64.0
LANES = 128
VMEM = pl.BlockSpec(memory_space=pltpu.VMEM)
SMEM = pl.BlockSpec(memory_space=pltpu.SMEM)
HBM = pl.BlockSpec(memory_space=pltpu.HBM)
LOADS = 4
LIMIT = pltpu.CompilerParams(vmem_limit_bytes=16 * 2**20)
ALL = pltpu.CompilerParams(vmem_limit_bytes=60 * 2**20)


def prepare_kernel(include_ref, groups_ref, linear_ref):
    fields = include_ref.shape[0]
    slots = groups_ref.shape[1]
    f32 = jnp.float32

    def dot(a, b, over):
        return lax.dot_general(
            a.astype(jnp.bfloat16),
            b.astype(jnp.bfloat16),
            ((over[:1], over[1:]), ((), ())),
            preferred_element_type=f32,
        )

    row = lax.broadcasted_iota(jnp.int32, (fields, fields), 0)
    column = lax.broadcasted_iota(jnp.int32, (fields, fields), 1)
    upper = jnp.where(column > row, 1.0, 0.0)
    lower = jnp.where(column < row, 1.0, 0.0)
    eye = jnp.where(column == row, 1.0, 0.0)
    included = jnp.where(column > row, include_ref[...], 0).astype(f32)
    place = dot(included, upper, (1, 0))
    both = included + dot(included, eye, (0, 0))
    count = jnp.sum(included, axis=1, keepdims=True)
    degree = jnp.sum(both, axis=1, keepdims=True)
    groups = jnp.floor((count + (PARTNERS - 1)) * (1.0 / PARTNERS))
    start = dot(lower, jnp.broadcast_to(groups, (fields, LANES)), (1, 0))[:, :1]
    total = jnp.sum(groups, axis=0, keepdims=True)
    slot = lax.broadcasted_iota(jnp.int32, (fields, slots), 1).astype(f32)
    ids = lax.broadcasted_iota(jnp.int32, (fields, slots), 0).astype(f32)
    inside = jnp.where((slot >= start) & (slot < start + groups), 1.0, 0.0)
    used = jnp.sum(inside, axis=0, keepdims=True)
    own = jnp.sum(inside * ids, axis=0, keepdims=True)
    first = jnp.sum(inside * (slot - start) * PARTNERS, axis=0, keepdims=True)
    places = dot(jnp.where(included > 0, place, -8.0), inside, (0, 0))
    places = jnp.where(used > 0, places, -8.0)
    groups_ref[...] = jnp.zeros(groups_ref.shape, jnp.int32)
    for u in range(PARTNERS):
        hit = jnp.where(places == first + u, 1.0, 0.0)
        found = jnp.sum(hit, axis=0, keepdims=True)
        partner = jnp.sum(hit * ids, axis=0, keepdims=True)
        absent = jnp.where(used > 0, float(fields), float(fields + 1))
        groups_ref[u : u + 1, :] = jnp.where(found > 0, partner, absent).astype(jnp.int32)
    owner = jnp.where(used > 0, own, float(fields + 1))
    groups_ref[PARTNERS : PARTNERS + 1, :] = owner.astype(jnp.int32)
    groups_ref[PARTNERS + 1 : PARTNERS + 2, :] = jnp.broadcast_to(total, (1, slots)).astype(
        jnp.int32
    )
    lanes = linear_ref.shape[1]
    padding = 2.0 * (groups * PARTNERS - count)
    wide = jnp.concatenate([both, jnp.zeros((fields, lanes - fields), f32)], axis=1)
    row = lax.broadcasted_iota(jnp.int32, (fields, lanes), 0)
    column = lax.broadcasted_iota(jnp.int32, (fields, lanes), 1)
    linear_ref[...] = jnp.where(row == column, 0.0, degree + wide) + padding


def prepare(pair_include):
    fields = pair_include.shape[0]
    most = sum(pl.cdiv(fields - 1 - a, PARTNERS) for a in range(fields))
    slots = pl.cdiv(most + 8, LANES) * LANES
    groups, linear = pl.pallas_call(
        prepare_kernel,
        out_shape=(
            jax.ShapeDtypeStruct((8, slots), jnp.int32),
            jax.ShapeDtypeStruct((fields, LANES), jnp.float32),
        ),
        compiler_params=LIMIT,
        name="prepare",
    )(pair_include)
    return groups.T.reshape(-1), linear


def factors_kernel(labels_ref, linear_ref, out_ref):
    turns, fields, band, width = out_ref.shape

    def one(field, carry):
        table = jnp.broadcast_to(linear_ref[pl.ds(field, 1), :], (band, LANES))
        for t in range(turns):
            mine = labels_ref[t * band : (t + 1) * band, :]
            factor = jnp.concatenate(
                [
                    jnp.take_along_axis(table, mine[:, at : at + LANES], axis=1)
                    for at in range(0, width, LANES)
                ],
                axis=1,
            )
            out_ref[t, field] = factor.astype(jnp.bfloat16)
        return carry

    lax.fori_loop(0, fields, one, 0, unroll=4)


def pairs_kernel(base_ref, groups_ref, *refs, scale, unroll, at_turn, label_turn):
    *parts, labels_ref, factors_ref, out_ref, held = refs
    fields = factors_ref.shape[1]
    _, each, rows, width = parts[0].shape
    held[fields] = jnp.full((rows, width), LOW, jnp.float32)
    held[fields + 1] = jnp.zeros((rows, width), jnp.float32)
    labels = labels_ref[...]
    linear = jnp.zeros((rows, width), jnp.float32)
    for k, part in enumerate(parts):
        for i in range(each):
            field = base_ref[k] + i
            values = jnp.where(labels == field, LOW, part[at_turn, i].astype(jnp.float32))
            held[field] = values
            linear = linear + factors_ref[label_turn, field].astype(jnp.float32) * values

    def step(number, total):
        for v in range(unroll):
            at = (number * unroll + v) * 8
            own = held[groups_ref[at + PARTNERS]]
            for u in range(PARTNERS):
                total = total + jnp.maximum(own, held[groups_ref[at + u]])
        return total

    steps = (groups_ref[PARTNERS + 1] + (unroll - 1)) // unroll
    total = lax.fori_loop(0, steps, step, jnp.zeros((rows, width), jnp.float32))
    out_ref[...] = (2.0 * total - linear) * scale


def pairs(base, groups, parts, labels, factors, at_turn, label_turn):
    fields = factors.shape[1]
    work = fields * fields * labels.size
    return pl.pallas_call(
        functools.partial(
            pairs_kernel,
            scale=2.0 / (fields * (fields - 1)),
            unroll=8,
            at_turn=at_turn,
            label_turn=label_turn,
        ),
        in_specs=[SMEM, SMEM] + [VMEM] * (len(parts) + 2),
        out_specs=VMEM,
        out_shape=jax.ShapeDtypeStruct(labels.shape, jnp.float32),
        scratch_shapes=[pltpu.VMEM((fields + 2, *labels.shape), jnp.float32)],
        compiler_params=LIMIT,
        cost_estimate=pl.CostEstimate(flops=work, bytes_accessed=work // 16, transcendentals=0),
        name="pairs",
    )(base, groups, *parts, labels, factors)


def load_fields(potentials_ref, held, sems):
    each = held.shape[0]
    step = max(each // LOADS, 1)
    copies = []
    for number, at in enumerate(range(0, each, step)):
        span = pl.ds(at, step)
        copies.append(
            pltpu.make_async_copy(potentials_ref.at[span], held.at[span], sems.at[number])
        )
        copies[-1].start()
    for number, copy in enumerate(copies):
        copy.wait()
        yield from range(number * step, (number + 1) * step)


def down_kernel(first_ref, potentials_ref, *refs):
    *outs, edge_ref, held, sems = refs
    _, height, width = held.shape
    turns, _, rows, _ = outs[0].shape
    row = lax.broadcasted_iota(jnp.int32, (rows, width), 0)
    lane = lax.broadcasted_iota(jnp.int32, (height, LANES), 1)
    for i in load_fields(potentials_ref, held, sems):
        for k, out in enumerate(outs):
            for t in range(turns):
                first = pl.multiple_of(first_ref[k * turns + t] * rows, rows)
                following = pl.multiple_of(jnp.minimum(first + rows, height - 8), 8)
                at_end = first + rows == height
                here = held[i, pl.ds(first, rows), :]
                below = held[i, pl.ds(following, 8), :]
                below = jnp.concatenate([here[1:], below[:1]], axis=0)
                change = jnp.where((row == rows - 1) & at_end, 0.0, below - here)
                out[t, i] = change.astype(jnp.bfloat16)
        edge_ref[...] = jnp.where(lane == i, held[i, :, 0:1], edge_ref[...] if i else 0.0)


def side_kernel(first_ref, potentials_ref, beside_ref, *outs, turns):
    _, each, rows, width = outs[0].shape
    parts = len(outs) // turns
    lane = lax.broadcasted_iota(jnp.int32, (rows, width), 1)
    at_end = first_ref[len(outs)] == 1
    for k in range(parts):
        for t in range(turns):
            first = pl.multiple_of(first_ref[k * turns + t] * rows, rows)
            for i in range(each):
                here = potentials_ref[i, pl.ds(first, rows), :]
                right = pltpu.roll(here, width - 1, 1)
                beside = beside_ref[pl.ds(first, rows), i : i + 1]
                right = jnp.where(lane == width - 1, beside, right)
                change = jnp.where((lane == width - 1) & at_end, 0.0, right - here)
                outs[t * parts + k][0, i] = change.astype(jnp.bfloat16)


def on_tile(body, name, out_shape, scalars, *arrays, fields=None):
    work = sum(a.size for a in arrays)
    specs = [VMEM] * len(arrays)
    scratch = []
    if fields is not None:
        arrays, specs = (fields, *arrays), [HBM, *specs]
        scratch = [pltpu.VMEM(fields.shape, fields.dtype), pltpu.SemaphoreType.DMA((LOADS,))]
        work = 2 * fields.size
    return pl.pallas_call(
        body,
        in_specs=[SMEM] * len(scalars) + specs,
        out_specs=jax.tree.map(lambda _: VMEM, out_shape),
        out_shape=out_shape,
        scratch_shapes=scratch,
        compiler_params=LIMIT if fields is None else ALL,
        cost_estimate=pl.CostEstimate(
            flops=4 * work, bytes_accessed=6 * work, transcendentals=0
        ),
        name=name,
    )(*scalars, *arrays)


def finish_kernel(halves_ref, *refs, chunks, width):
    *pieces, across, down, out_across, out_down = refs
    for (turn, contents), piece in zip(chunks, pieces):
        lanes = pl.ds(pl.multiple_of(halves_ref[turn] * width, width), width)
        at = 0
        for kind, first, rows in contents:
            conduct, out = (down, out_down) if kind == "down" else (across, out_across)
            out[first : first + rows, lanes] = (
                conduct[first : first + rows, lanes] * piece[at : at + rows]
            )
            at += rows


def finish(chunks, halves, pieces, conduct_across, conduct_down):
    shape = jax.ShapeDtypeStruct(conduct_across.shape, jnp.float32)
    return pl.pallas_call(
        functools.partial(finish_kernel, chunks=chunks, width=pieces[0].shape[1]),
        in_specs=[SMEM] + [VMEM] * (len(pieces) + 2),
        out_specs=[VMEM, VMEM],
        out_shape=[shape, shape],
        compiler_params=LIMIT,
        name="finish",
    )(halves, *pieces, conduct_across, conduct_down)


def after(value, *others):
    return lax.optimization_barrier((value, *others))[0]


def towards(index, step, size):
    return index ^ step if size & (size - 1) == 0 else (index + step) % size


def source(index, step, size):
    return index ^ step if size & (size - 1) == 0 else (index + size - step) % size


def local(potentials, pair_include, labels, conduct_across, conduct_down):
    parts, strips = lax.axis_size("cores"), lax.axis_size("strip")
    core, strip = lax.axis_index("cores"), lax.axis_index("strip")
    each, height, width = potentials.shape
    rows = labels.shape[0]
    turns = strips // parts

    flat = [(c, s // turns, s % turns) for c in range(parts) for s in range(strips)]

    def number(c, group, j):
        return c * strips + group * turns + j

    def move(array, to):
        moves = [(number(*at), number(*to(*at))) for at in flat]
        return lax.ppermute(array, ("cores", "strip"), moves)

    def send_home(array, turn):
        return move(array, lambda c, g, j: (g, c, towards(j, turn, turns)))

    def exchange(block, k):
        moves = [(i, towards(i, k, parts)) for i in range(parts)]
        return lax.ppermute(block, "cores", moves)

    inside = strip % turns
    ts = jnp.arange(turns, dtype=jnp.int32)
    ks = jnp.arange(parts, dtype=jnp.int32)
    base = source(core, ks, parts) * each
    first = towards(core, ks, parts)[:, None] * turns + towards(inside, ts, turns)[None]
    last = (strip == strips - 1).astype(jnp.int32)
    first = jnp.concatenate([first.reshape(-1), last[None]])
    halves = source(inside, ts, turns)

    block = jax.ShapeDtypeStruct((turns, each, rows, width), jnp.bfloat16)
    column = jax.ShapeDtypeStruct((height, LANES), jnp.float32)
    *down, edge = on_tile(
        down_kernel, "down", [block] * parts + [column], [first], fields=potentials
    )
    far = list(range(parts - 1, 0, -1))
    down = [down[0], *[exchange(down[k], k) for k in far][::-1]]
    beside = lax.ppermute(edge, "strip", [(i, i - 1) for i in range(1, strips)])
    labels = move(after(labels, edge), lambda c, g, j: (g, c, j))
    groups, linear = prepare(after(pair_include, edge))

    own_labels = []
    for t in range(turns):
        to = towards(inside, t, turns)
        part = lax.dynamic_slice_in_dim(labels, to * width, width, 1)
        back = (turns - t) % turns if turns & (turns - 1) else t
        own_labels.append((back, move(part, lambda c, g, j: (c, g, towards(j, t, turns))) if t else part))
    own_labels = [part for _, part in sorted(own_labels, key=lambda pair: pair[0])]

    block = jax.ShapeDtypeStruct((1, each, rows, width), jnp.bfloat16)
    side = on_tile(
        functools.partial(side_kernel, turns=turns),
        "side",
        [block] * (parts * turns),
        [after(first, *own_labels, groups)],
        potentials,
        beside,
    )
    factors = on_tile(
        factors_kernel,
        "factors",
        jax.ShapeDtypeStruct((turns, parts * each, rows, width), jnp.bfloat16),
        [],
        jnp.concatenate(own_labels, axis=0),
        after(linear, *side),
    )
    blocks = [side[t * parts : (t + 1) * parts] for t in range(turns)]
    def band_sums(t, got):
        return pairs(base, groups, got, own_labels[t], factors, t, t)

    down[0] = after(down[0], *down[1:])
    down_sums = [band_sums(0, down)]
    arrived = []
    for t in range(turns):
        got = [blocks[t][0]]
        for k in far:
            waits = [] if t == 0 else down_sums[-1:]
            got.insert(1, exchange(after(blocks[t][k], *waits), k))
        arrived.append(got)
    down[0] = after(down[0], arrived[0][1])
    down_sums += [band_sums(t, down) for t in range(1, turns)]
    side_sums, pieces = [], []
    for t in range(turns):
        got = arrived[t]
        got[0] = after(got[0], (side_sums or down_sums)[-1])
        side_sums.append(pairs(base, groups, got, own_labels[t], factors, 0, t))
        joined = jnp.concatenate([down_sums[t], side_sums[t]], axis=0)
        pieces.append(send_home(joined, t))
    contents = tuple((t, (("down", 0, rows), ("side", 0, rows))) for t in range(turns))
    return finish(contents, halves, pieces, conduct_across, conduct_down)


def solution(mesh):
    return jax.shard_map(
        local,
        mesh=mesh,
        in_specs=(
            P("cores", None, "strip"),
            P(),
            P("strip", "cores"),
            P("strip", "cores"),
            P("strip", "cores"),
        ),
        out_specs=(P("strip", "cores"), P("strip", "cores")),
        check_vma=False,
    )
```

```python
import functools

import jax
import jax.numpy as jnp
from jax import lax
from jax.experimental import pallas as pl
from jax.experimental.pallas import tpu as pltpu
from jax.sharding import PartitionSpec as P

PARTNERS = 4
LOW = -64.0
LANES = 128
VMEM = pl.BlockSpec(memory_space=pltpu.VMEM)
SMEM = pl.BlockSpec(memory_space=pltpu.SMEM)
HBM = pl.BlockSpec(memory_space=pltpu.HBM)
LOADS = 4
LIMIT = pltpu.CompilerParams(vmem_limit_bytes=16 * 2**20)
ALL = pltpu.CompilerParams(vmem_limit_bytes=60 * 2**20)


def prepare_kernel(include_ref, groups_ref, linear_ref):
    fields = include_ref.shape[0]
    slots = groups_ref.shape[1]
    f32 = jnp.float32

    def dot(a, b, over):
        return lax.dot_general(
            a.astype(jnp.bfloat16),
            b.astype(jnp.bfloat16),
            ((over[:1], over[1:]), ((), ())),
            preferred_element_type=f32,
        )

    row = lax.broadcasted_iota(jnp.int32, (fields, fields), 0)
    column = lax.broadcasted_iota(jnp.int32, (fields, fields), 1)
    upper = jnp.where(column > row, 1.0, 0.0)
    lower = jnp.where(column < row, 1.0, 0.0)
    eye = jnp.where(column == row, 1.0, 0.0)
    included = jnp.where(column > row, include_ref[...], 0).astype(f32)
    both = included + dot(included, eye, (0, 0))
    many = jnp.sum(jnp.sum(included, axis=1, keepdims=True), axis=0, keepdims=True)
    rest = jnp.where(many > fields * (fields - 1) / 4, 1.0, 0.0)
    listed = jnp.where(rest > 0, upper - included, included)
    place = dot(listed, upper, (1, 0))
    count = jnp.sum(listed, axis=1, keepdims=True)
    degree = jnp.sum(both, axis=1, keepdims=True)
    groups = jnp.floor((count + (PARTNERS - 1)) * (1.0 / PARTNERS))
    start = dot(lower, jnp.broadcast_to(groups, (fields, LANES)), (1, 0))[:, :1]
    total = jnp.sum(groups, axis=0, keepdims=True)
    slot = lax.broadcasted_iota(jnp.int32, (fields, slots), 1).astype(f32)
    ids = lax.broadcasted_iota(jnp.int32, (fields, slots), 0).astype(f32)
    inside = jnp.where((slot >= start) & (slot < start + groups), 1.0, 0.0)
    used = jnp.sum(inside, axis=0, keepdims=True)
    own = jnp.sum(inside * ids, axis=0, keepdims=True)
    first = jnp.sum(inside * (slot - start) * PARTNERS, axis=0, keepdims=True)
    places = dot(jnp.where(listed > 0, place, -8.0), inside, (0, 0))
    places = jnp.where(used > 0, places, -8.0)
    groups_ref[...] = jnp.zeros(groups_ref.shape, jnp.int32)
    for u in range(PARTNERS):
        hit = jnp.where(places == first + u, 1.0, 0.0)
        found = jnp.sum(hit, axis=0, keepdims=True)
        partner = jnp.sum(hit * ids, axis=0, keepdims=True)
        absent = jnp.where(used > 0, float(fields), float(fields + 1))
        groups_ref[u : u + 1, :] = jnp.where(found > 0, partner, absent).astype(jnp.int32)
    owner = jnp.where(used > 0, own, float(fields + 1))
    groups_ref[PARTNERS : PARTNERS + 1, :] = owner.astype(jnp.int32)
    groups_ref[PARTNERS + 1 : PARTNERS + 2, :] = jnp.broadcast_to(total, (1, slots)).astype(
        jnp.int32
    )
    groups_ref[PARTNERS + 2 : PARTNERS + 3, :] = jnp.broadcast_to(rest, (1, slots)).astype(
        jnp.int32
    )
    lanes = linear_ref.shape[1]
    padding = (2.0 - 4.0 * rest) * (groups * PARTNERS - count)
    wide = jnp.concatenate([both, jnp.zeros((fields, lanes - fields), f32)], axis=1)
    row = lax.broadcasted_iota(jnp.int32, (fields, lanes), 0)
    column = lax.broadcasted_iota(jnp.int32, (fields, lanes), 1)
    linear_ref[...] = jnp.where(row == column, 0.0, degree + wide) + padding


def prepare(pair_include):
    fields = pair_include.shape[0]
    most = sum(pl.cdiv(fields - 1 - a, PARTNERS) for a in range(fields))
    slots = pl.cdiv(most + 8, LANES) * LANES
    groups, linear = pl.pallas_call(
        prepare_kernel,
        out_shape=(
            jax.ShapeDtypeStruct((8, slots), jnp.int32),
            jax.ShapeDtypeStruct((fields, LANES), jnp.float32),
        ),
        compiler_params=LIMIT,
        name="prepare",
    )(pair_include)
    return groups.T.reshape(-1), linear


def factors_kernel(labels_ref, linear_ref, out_ref):
    turns, fields, band, width = out_ref.shape

    def one(field, carry):
        table = jnp.broadcast_to(linear_ref[pl.ds(field, 1), :], (band, LANES))
        for t in range(turns):
            mine = labels_ref[t * band : (t + 1) * band, :]
            factor = jnp.concatenate(
                [
                    jnp.take_along_axis(table, mine[:, at : at + LANES], axis=1)
                    for at in range(0, width, LANES)
                ],
                axis=1,
            )
            out_ref[t, field] = factor.astype(jnp.bfloat16)
        return carry

    lax.fori_loop(0, fields, one, 0, unroll=4)


def sort_steps(size):
    p = 1
    while p < size:
        k = p
        while k >= 1:
            for j in range(k % p, size - k, 2 * k):
                for i in range(min(k, size - j - k)):
                    if (i + j) // (2 * p) == (i + j + k) // (2 * p):
                        yield i + j, i + j + k
            k //= 2
        p *= 2


def compare(values, steps):
    for i, j in steps:
        low = jnp.minimum(values[i], values[j])
        values[j] = jnp.maximum(values[i], values[j])
        values[i] = low
    return values


def merge_steps(size):
    k = size // 2
    while k >= 1:
        for i in range(size):
            if not i & k:
                yield i, i + k
        k //= 2


def rank_sums(ranked, out_ref):
    fields, rows, width = ranked.shape
    half = fields // 2
    columns = width // LANES

    def block(number, carry):
        place = (
            pl.ds(pl.multiple_of(number // columns * 16, 16), 16),
            pl.ds(pl.multiple_of(number % columns * LANES, LANES), LANES),
        )
        for start in (0, half):
            values = [ranked[(start + i, *place)] for i in range(half)]
            for i, value in enumerate(compare(values, sort_steps(half))):
                ranked[(start + i, *place)] = value
        total = jnp.zeros((16, LANES), jnp.float32)
        for start, pick in ((0, jnp.minimum), (half, jnp.maximum)):
            values = [
                pick(ranked[(i, *place)], ranked[(fields - 1 - i, *place)]) for i in range(half)
            ]
            for i, value in enumerate(compare(values, merge_steps(half))):
                if start + i:
                    total = total + value.astype(jnp.float32) * float(start + i)
        out_ref[place] = total
        return carry

    lax.fori_loop(0, rows // 16 * columns, block, 0)


def pairs_kernel(base_ref, groups_ref, *refs, scale, unroll, at_turn, label_turn):
    *parts, labels_ref, factors_ref, out_ref, held, ranked = refs
    fields = factors_ref.shape[1]
    _, each, rows, width = parts[0].shape
    held[fields] = jnp.full((rows, width), LOW, jnp.float32)
    held[fields + 1] = jnp.zeros((rows, width), jnp.float32)
    labels = labels_ref[...]
    linear = jnp.zeros((rows, width), jnp.float32)
    for k, part in enumerate(parts):
        for i in range(each):
            field = base_ref[k] + i
            values = jnp.where(labels == field, LOW, part[at_turn, i].astype(jnp.float32))
            held[field] = values
            ranked[k * each + i] = values.astype(jnp.bfloat16)
            linear = linear + factors_ref[label_turn, field].astype(jnp.float32) * values

    out_ref[...] = jnp.zeros((rows, width), jnp.float32)

    @pl.when(groups_ref[PARTNERS + 2] == 1)
    def _():
        rank_sums(ranked, out_ref)

    def step(number, total):
        for v in range(unroll):
            at = (number * unroll + v) * 8
            own = held[groups_ref[at + PARTNERS]]
            for u in range(PARTNERS):
                total = total + jnp.maximum(own, held[groups_ref[at + u]])
        return total

    steps = (groups_ref[PARTNERS + 1] + (unroll - 1)) // unroll
    total = lax.fori_loop(0, steps, step, jnp.zeros((rows, width), jnp.float32))
    sign = 1.0 - 2.0 * groups_ref[PARTNERS + 2].astype(jnp.float32)
    out_ref[...] = (2.0 * (out_ref[...] + sign * total) - linear) * scale


def pairs(base, groups, parts, labels, factors, at_turn, label_turn):
    fields = factors.shape[1]
    work = fields * fields * labels.size
    return pl.pallas_call(
        functools.partial(
            pairs_kernel,
            scale=2.0 / (fields * (fields - 1)),
            unroll=8,
            at_turn=at_turn,
            label_turn=label_turn,
        ),
        in_specs=[SMEM, SMEM] + [VMEM] * (len(parts) + 2),
        out_specs=VMEM,
        out_shape=jax.ShapeDtypeStruct(labels.shape, jnp.float32),
        scratch_shapes=[
            pltpu.VMEM((fields + 2, *labels.shape), jnp.float32),
            pltpu.VMEM((fields, *labels.shape), jnp.bfloat16),
        ],
        compiler_params=LIMIT,
        cost_estimate=pl.CostEstimate(flops=work, bytes_accessed=work // 16, transcendentals=0),
        name="pairs",
    )(base, groups, *parts, labels, factors)


def load_fields(potentials_ref, held, sems):
    each = held.shape[0]
    step = max(each // LOADS, 1)
    copies = []
    for number, at in enumerate(range(0, each, step)):
        span = pl.ds(at, step)
        copies.append(
            pltpu.make_async_copy(potentials_ref.at[span], held.at[span], sems.at[number])
        )
        copies[-1].start()
    for number, copy in enumerate(copies):
        copy.wait()
        yield from range(number * step, (number + 1) * step)


def down_kernel(first_ref, potentials_ref, *refs):
    *outs, edge_ref, held, sems = refs
    _, height, width = held.shape
    turns, _, rows, _ = outs[0].shape
    row = lax.broadcasted_iota(jnp.int32, (rows, width), 0)
    lane = lax.broadcasted_iota(jnp.int32, (height, LANES), 1)
    for i in load_fields(potentials_ref, held, sems):
        for k, out in enumerate(outs):
            for t in range(turns):
                first = pl.multiple_of(first_ref[k * turns + t] * rows, rows)
                following = pl.multiple_of(jnp.minimum(first + rows, height - 8), 8)
                at_end = first + rows == height
                here = held[i, pl.ds(first, rows), :]
                below = held[i, pl.ds(following, 8), :]
                below = jnp.concatenate([here[1:], below[:1]], axis=0)
                change = jnp.where((row == rows - 1) & at_end, 0.0, below - here)
                out[t, i] = change.astype(jnp.bfloat16)
        edge_ref[...] = jnp.where(lane == i, held[i, :, 0:1], edge_ref[...] if i else 0.0)


def side_kernel(first_ref, potentials_ref, beside_ref, *outs, turns):
    _, each, rows, width = outs[0].shape
    parts = len(outs) // turns
    lane = lax.broadcasted_iota(jnp.int32, (rows, width), 1)
    at_end = first_ref[len(outs)] == 1
    for k in range(parts):
        for t in range(turns):
            first = pl.multiple_of(first_ref[k * turns + t] * rows, rows)
            for i in range(each):
                here = potentials_ref[i, pl.ds(first, rows), :]
                right = pltpu.roll(here, width - 1, 1)
                beside = beside_ref[pl.ds(first, rows), i : i + 1]
                right = jnp.where(lane == width - 1, beside, right)
                change = jnp.where((lane == width - 1) & at_end, 0.0, right - here)
                outs[t * parts + k][0, i] = change.astype(jnp.bfloat16)


def on_tile(body, name, out_shape, scalars, *arrays, fields=None):
    work = sum(a.size for a in arrays)
    specs = [VMEM] * len(arrays)
    scratch = []
    if fields is not None:
        arrays, specs = (fields, *arrays), [HBM, *specs]
        scratch = [pltpu.VMEM(fields.shape, fields.dtype), pltpu.SemaphoreType.DMA((LOADS,))]
        work = 2 * fields.size
    return pl.pallas_call(
        body,
        in_specs=[SMEM] * len(scalars) + specs,
        out_specs=jax.tree.map(lambda _: VMEM, out_shape),
        out_shape=out_shape,
        scratch_shapes=scratch,
        compiler_params=LIMIT if fields is None else ALL,
        cost_estimate=pl.CostEstimate(
            flops=4 * work, bytes_accessed=6 * work, transcendentals=0
        ),
        name=name,
    )(*scalars, *arrays)


def finish_kernel(halves_ref, *refs, chunks, width):
    *pieces, across, down, out_across, out_down = refs
    for (turn, contents), piece in zip(chunks, pieces):
        lanes = pl.ds(pl.multiple_of(halves_ref[turn] * width, width), width)
        at = 0
        for kind, first, rows in contents:
            conduct, out = (down, out_down) if kind == "down" else (across, out_across)
            out[first : first + rows, lanes] = (
                conduct[first : first + rows, lanes] * piece[at : at + rows]
            )
            at += rows


def finish(chunks, halves, pieces, conduct_across, conduct_down):
    shape = jax.ShapeDtypeStruct(conduct_across.shape, jnp.float32)
    return pl.pallas_call(
        functools.partial(finish_kernel, chunks=chunks, width=pieces[0].shape[1]),
        in_specs=[SMEM] + [VMEM] * (len(pieces) + 2),
        out_specs=[VMEM, VMEM],
        out_shape=[shape, shape],
        compiler_params=LIMIT,
        name="finish",
    )(halves, *pieces, conduct_across, conduct_down)


def after(value, *others):
    return lax.optimization_barrier((value, *others))[0]


def towards(index, step, size):
    return index ^ step if size & (size - 1) == 0 else (index + step) % size


def source(index, step, size):
    return index ^ step if size & (size - 1) == 0 else (index + size - step) % size


def local(potentials, pair_include, labels, conduct_across, conduct_down):
    parts, strips = lax.axis_size("cores"), lax.axis_size("strip")
    core, strip = lax.axis_index("cores"), lax.axis_index("strip")
    each, height, width = potentials.shape
    rows = labels.shape[0]
    turns = strips // parts

    flat = [(c, s // turns, s % turns) for c in range(parts) for s in range(strips)]

    def number(c, group, j):
        return c * strips + group * turns + j

    def move(array, to):
        moves = [(number(*at), number(*to(*at))) for at in flat]
        return lax.ppermute(array, ("cores", "strip"), moves)

    def send_home(array, turn):
        return move(
            array, lambda c, g, j: (g, towards(c, g, parts), towards(j, turn, turns))
        )

    def exchange(block, k):
        moves = [(i, towards(i, k, parts)) for i in range(parts)]
        return lax.ppermute(block, "cores", moves)

    inside = strip % turns
    ts = jnp.arange(turns, dtype=jnp.int32)
    ks = jnp.arange(parts, dtype=jnp.int32)
    base = source(core, ks, parts) * each
    region = towards(towards(core, ks, parts), strip // turns, parts)
    first = region[:, None] * turns + towards(inside, ts, turns)[None]
    last = (strip == strips - 1).astype(jnp.int32)
    first = jnp.concatenate([first.reshape(-1), last[None]])
    halves = source(inside, ts, turns)

    block = jax.ShapeDtypeStruct((turns, each, rows, width), jnp.bfloat16)
    column = jax.ShapeDtypeStruct((height, LANES), jnp.float32)
    *down, edge = on_tile(
        down_kernel, "down", [block] * parts + [column], [first], fields=potentials
    )
    far = list(range(parts - 1, 0, -1))
    beside = lax.ppermute(edge, "strip", [(i, i - 1) for i in range(1, strips)])
    labels = move(labels, lambda c, g, j: (source(g, c, parts), c, j))
    down = after(tuple(down), labels)
    down = [down[0], *[exchange(down[k], k) for k in far][::-1]]
    groups, linear = prepare(after(pair_include, edge))

    own_labels = []
    for t in range(turns):
        to = towards(inside, t, turns)
        part = lax.dynamic_slice_in_dim(labels, to * width, width, 1)
        back = (turns - t) % turns if turns & (turns - 1) else t
        own_labels.append((back, move(part, lambda c, g, j: (c, g, towards(j, t, turns))) if t else part))
    own_labels = [part for _, part in sorted(own_labels, key=lambda pair: pair[0])]

    block = jax.ShapeDtypeStruct((1, each, rows, width), jnp.bfloat16)
    side = on_tile(
        functools.partial(side_kernel, turns=turns),
        "side",
        [block] * (parts * turns),
        [after(first, *own_labels, groups)],
        potentials,
        beside,
    )
    factors = on_tile(
        factors_kernel,
        "factors",
        jax.ShapeDtypeStruct((turns, parts * each, rows, width), jnp.bfloat16),
        [],
        jnp.concatenate(own_labels, axis=0),
        after(linear, *side),
    )
    blocks = [side[t * parts : (t + 1) * parts] for t in range(turns)]
    def band_sums(t, got):
        return pairs(base, groups, got, own_labels[t], factors, t, t)

    down[0] = after(down[0], *down[1:])
    down_sums = [band_sums(0, down)]
    arrived = []
    for t in range(turns):
        got = [blocks[t][0]]
        for k in far:
            waits = [factors] if t == 0 else down_sums[-1:]
            got.insert(1, exchange(after(blocks[t][k], *waits), k))
        arrived.append(got)
    down[0] = after(down[0], arrived[0][1])
    down_sums += [band_sums(t, down) for t in range(1, turns)]
    side_sums, pieces = [], []
    for t in range(turns):
        got = arrived[t]
        got[0] = after(got[0], (side_sums or down_sums)[-1])
        side_sums.append(pairs(base, groups, got, own_labels[t], factors, 0, t))
        joined = jnp.concatenate([down_sums[t], side_sums[t]], axis=0)
        pieces.append(send_home(joined, t))
    contents = tuple((t, (("down", 0, rows), ("side", 0, rows))) for t in range(turns))
    return finish(contents, halves, pieces, conduct_across, conduct_down)


def solution(mesh):
    return jax.shard_map(
        local,
        mesh=mesh,
        in_specs=(
            P("cores", None, "strip"),
            P(),
            P("strip", "cores"),
            P("strip", "cores"),
            P("strip", "cores"),
        ),
        out_specs=(P("strip", "cores"), P("strip", "cores")),
        check_vma=False,
    )
```

```python
import functools

import jax
import jax.numpy as jnp
from jax import lax
from jax.experimental import pallas as pl
from jax.experimental.pallas import tpu as pltpu
from jax.sharding import PartitionSpec as P

PARTNERS = 4
LOW = -64.0
LANES = 128
VMEM = pl.BlockSpec(memory_space=pltpu.VMEM)
SMEM = pl.BlockSpec(memory_space=pltpu.SMEM)
HBM = pl.BlockSpec(memory_space=pltpu.HBM)
LOADS = 4
LIMIT = pltpu.CompilerParams(vmem_limit_bytes=16 * 2**20)
ALL = pltpu.CompilerParams(vmem_limit_bytes=60 * 2**20)


def prepare_kernel(include_ref, groups_ref, linear_ref):
    fields = include_ref.shape[0]
    slots = groups_ref.shape[1]
    f32 = jnp.float32

    def dot(a, b, over):
        return lax.dot_general(
            a.astype(jnp.bfloat16),
            b.astype(jnp.bfloat16),
            ((over[:1], over[1:]), ((), ())),
            preferred_element_type=f32,
        )

    row = lax.broadcasted_iota(jnp.int32, (fields, fields), 0)
    column = lax.broadcasted_iota(jnp.int32, (fields, fields), 1)
    upper = jnp.where(column > row, 1.0, 0.0)
    lower = jnp.where(column < row, 1.0, 0.0)
    eye = jnp.where(column == row, 1.0, 0.0)
    included = jnp.where(column > row, include_ref[...], 0).astype(f32)
    both = included + dot(included, eye, (0, 0))
    many = jnp.sum(jnp.sum(included, axis=1, keepdims=True), axis=0, keepdims=True)
    rest = jnp.where(many > fields * (fields - 1) / 4, 1.0, 0.0)
    listed = jnp.where(rest > 0, upper - included, included)
    place = dot(listed, upper, (1, 0))
    count = jnp.sum(listed, axis=1, keepdims=True)
    degree = jnp.sum(both, axis=1, keepdims=True)
    groups = jnp.floor((count + (PARTNERS - 1)) * (1.0 / PARTNERS))
    start = dot(lower, jnp.broadcast_to(groups, (fields, LANES)), (1, 0))[:, :1]
    total = jnp.sum(groups, axis=0, keepdims=True)
    slot = lax.broadcasted_iota(jnp.int32, (fields, slots), 1).astype(f32)
    ids = lax.broadcasted_iota(jnp.int32, (fields, slots), 0).astype(f32)
    inside = jnp.where((slot >= start) & (slot < start + groups), 1.0, 0.0)
    used = jnp.sum(inside, axis=0, keepdims=True)
    own = jnp.sum(inside * ids, axis=0, keepdims=True)
    first = jnp.sum(inside * (slot - start) * PARTNERS, axis=0, keepdims=True)
    places = dot(jnp.where(listed > 0, place, -8.0), inside, (0, 0))
    places = jnp.where(used > 0, places, -8.0)
    groups_ref[...] = jnp.zeros(groups_ref.shape, jnp.int32)
    for u in range(PARTNERS):
        hit = jnp.where(places == first + u, 1.0, 0.0)
        found = jnp.sum(hit, axis=0, keepdims=True)
        partner = jnp.sum(hit * ids, axis=0, keepdims=True)
        absent = jnp.where(used > 0, float(fields), float(fields + 1))
        groups_ref[u : u + 1, :] = jnp.where(found > 0, partner, absent).astype(jnp.int32)
    owner = jnp.where(used > 0, own, float(fields + 1))
    groups_ref[PARTNERS : PARTNERS + 1, :] = owner.astype(jnp.int32)
    groups_ref[PARTNERS + 1 : PARTNERS + 2, :] = jnp.broadcast_to(total, (1, slots)).astype(
        jnp.int32
    )
    groups_ref[PARTNERS + 2 : PARTNERS + 3, :] = jnp.broadcast_to(rest, (1, slots)).astype(
        jnp.int32
    )
    lanes = linear_ref.shape[1]
    padding = (2.0 - 4.0 * rest) * (groups * PARTNERS - count)
    wide = jnp.concatenate([both, jnp.zeros((fields, lanes - fields), f32)], axis=1)
    row = lax.broadcasted_iota(jnp.int32, (fields, lanes), 0)
    column = lax.broadcasted_iota(jnp.int32, (fields, lanes), 1)
    linear_ref[...] = jnp.where(row == column, 0.0, degree + wide) + padding


def prepare(pair_include):
    fields = pair_include.shape[0]
    most = sum(pl.cdiv(fields - 1 - a, PARTNERS) for a in range(fields))
    slots = pl.cdiv(most + 8, LANES) * LANES
    groups, linear = pl.pallas_call(
        prepare_kernel,
        out_shape=(
            jax.ShapeDtypeStruct((8, slots), jnp.int32),
            jax.ShapeDtypeStruct((fields, LANES), jnp.float32),
        ),
        compiler_params=LIMIT,
        name="prepare",
    )(pair_include)
    return groups.T.reshape(-1), linear


def factors_kernel(labels_ref, linear_ref, out_ref):
    turns, fields, band, width = out_ref.shape

    def one(field, carry):
        table = jnp.broadcast_to(linear_ref[pl.ds(field, 1), :], (band, LANES))
        for t in range(turns):
            mine = labels_ref[t * band : (t + 1) * band, :]
            factor = jnp.concatenate(
                [
                    jnp.take_along_axis(table, mine[:, at : at + LANES], axis=1)
                    for at in range(0, width, LANES)
                ],
                axis=1,
            )
            out_ref[t, field] = factor.astype(jnp.bfloat16)
        return carry

    lax.fori_loop(0, fields, one, 0, unroll=4)


def sort_steps(size):
    p = 1
    while p < size:
        k = p
        while k >= 1:
            for j in range(k % p, size - k, 2 * k):
                for i in range(min(k, size - j - k)):
                    if (i + j) // (2 * p) == (i + j + k) // (2 * p):
                        yield i + j, i + j + k
            k //= 2
        p *= 2


def compare(values, steps):
    for i, j in steps:
        low = jnp.minimum(values[i], values[j])
        values[j] = jnp.maximum(values[i], values[j])
        values[i] = low
    return values


def merge_steps(size):
    k = size // 2
    while k >= 1:
        for i in range(size):
            if not i & k:
                yield i, i + k
        k //= 2


def rank_sums(held, ranked, out_ref):
    fields = ranked.shape[0]
    rows, width = out_ref.shape
    half = fields // 2
    columns = width // LANES

    def block(number, carry):
        place = (
            pl.ds(pl.multiple_of(number // columns * 8, 8), 8),
            pl.ds(pl.multiple_of(number % columns * LANES, LANES), LANES),
        )
        for start in (0, half):
            values = [held[(start + i, *place)] for i in range(half)]
            for i, value in enumerate(compare(values, sort_steps(half))):
                ranked[start + i] = value
        total = jnp.zeros((8, LANES), jnp.float32)
        for start, pick in ((0, jnp.minimum), (half, jnp.maximum)):
            values = [
                pick(ranked[i], ranked[fields - 1 - i]) for i in range(half)
            ]
            for i, value in enumerate(compare(values, merge_steps(half))):
                if start + i:
                    total = total + value * float(start + i)
        out_ref[place] = total
        return carry

    lax.fori_loop(0, rows // 8 * columns, block, 0)


def pairs_kernel(base_ref, groups_ref, *refs, scale, unroll, at_turn, label_turn):
    *parts, labels_ref, factors_ref, out_ref, held, ranked = refs
    fields = factors_ref.shape[1]
    _, each, rows, width = parts[0].shape
    held[fields] = jnp.full((rows, width), LOW, jnp.float32)
    held[fields + 1] = jnp.zeros((rows, width), jnp.float32)
    labels = labels_ref[...]
    linear = jnp.zeros((rows, width), jnp.float32)
    for k, part in enumerate(parts):
        for i in range(each):
            field = base_ref[k] + i
            values = jnp.where(labels == field, LOW, part[at_turn, i].astype(jnp.float32))
            held[field] = values
            linear = linear + factors_ref[label_turn, field].astype(jnp.float32) * values

    out_ref[...] = jnp.zeros((rows, width), jnp.float32)

    @pl.when(groups_ref[PARTNERS + 2] == 1)
    def _():
        rank_sums(held, ranked, out_ref)

    def step(number, total):
        for v in range(unroll):
            at = (number * unroll + v) * 8
            own = held[groups_ref[at + PARTNERS]]
            for u in range(PARTNERS):
                total = total + jnp.maximum(own, held[groups_ref[at + u]])
        return total

    steps = (groups_ref[PARTNERS + 1] + (unroll - 1)) // unroll
    total = lax.fori_loop(0, steps, step, jnp.zeros((rows, width), jnp.float32))
    sign = 1.0 - 2.0 * groups_ref[PARTNERS + 2].astype(jnp.float32)
    out_ref[...] = (2.0 * (out_ref[...] + sign * total) - linear) * scale


def pairs(base, groups, parts, labels, factors, at_turn, label_turn):
    fields = factors.shape[1]
    work = fields * fields * labels.size
    return pl.pallas_call(
        functools.partial(
            pairs_kernel,
            scale=2.0 / (fields * (fields - 1)),
            unroll=8,
            at_turn=at_turn,
            label_turn=label_turn,
        ),
        in_specs=[SMEM, SMEM] + [VMEM] * (len(parts) + 2),
        out_specs=VMEM,
        out_shape=jax.ShapeDtypeStruct(labels.shape, jnp.float32),
        scratch_shapes=[
            pltpu.VMEM((fields + 2, *labels.shape), jnp.float32),
            pltpu.VMEM((fields, 8, LANES), jnp.float32),
        ],
        compiler_params=LIMIT,
        cost_estimate=pl.CostEstimate(flops=work, bytes_accessed=work // 16, transcendentals=0),
        name="pairs",
    )(base, groups, *parts, labels, factors)


def load_fields(potentials_ref, held, sems):
    each = held.shape[0]
    step = max(each // LOADS, 1)
    copies = []
    for number, at in enumerate(range(0, each, step)):
        span = pl.ds(at, step)
        copies.append(
            pltpu.make_async_copy(potentials_ref.at[span], held.at[span], sems.at[number])
        )
        copies[-1].start()
    for number, copy in enumerate(copies):
        copy.wait()
        yield from range(number * step, (number + 1) * step)


def down_kernel(first_ref, potentials_ref, *refs):
    *outs, edge_ref, held, sems = refs
    _, height, width = held.shape
    turns, _, rows, _ = outs[0].shape
    row = lax.broadcasted_iota(jnp.int32, (rows, width), 0)
    lane = lax.broadcasted_iota(jnp.int32, (height, LANES), 1)
    for i in load_fields(potentials_ref, held, sems):
        for k, out in enumerate(outs):
            for t in range(turns):
                first = pl.multiple_of(first_ref[k * turns + t] * rows, rows)
                following = pl.multiple_of(jnp.minimum(first + rows, height - 8), 8)
                at_end = first + rows == height
                here = held[i, pl.ds(first, rows), :]
                below = held[i, pl.ds(following, 8), :]
                below = jnp.concatenate([here[1:], below[:1]], axis=0)
                change = jnp.where((row == rows - 1) & at_end, 0.0, below - here)
                out[t, i] = change.astype(jnp.bfloat16)
        edge_ref[...] = jnp.where(lane == i, held[i, :, 0:1], edge_ref[...] if i else 0.0)


def side_kernel(first_ref, potentials_ref, beside_ref, *outs, turns):
    _, each, rows, width = outs[0].shape
    parts = len(outs) // turns
    lane = lax.broadcasted_iota(jnp.int32, (rows, width), 1)
    at_end = first_ref[len(outs)] == 1
    for k in range(parts):
        for t in range(turns):
            first = pl.multiple_of(first_ref[k * turns + t] * rows, rows)
            for i in range(each):
                here = potentials_ref[i, pl.ds(first, rows), :]
                right = pltpu.roll(here, width - 1, 1)
                beside = beside_ref[pl.ds(first, rows), i : i + 1]
                right = jnp.where(lane == width - 1, beside, right)
                change = jnp.where((lane == width - 1) & at_end, 0.0, right - here)
                outs[t * parts + k][0, i] = change.astype(jnp.bfloat16)


def on_tile(body, name, out_shape, scalars, *arrays, fields=None):
    work = sum(a.size for a in arrays)
    specs = [VMEM] * len(arrays)
    scratch = []
    if fields is not None:
        arrays, specs = (fields, *arrays), [HBM, *specs]
        scratch = [pltpu.VMEM(fields.shape, fields.dtype), pltpu.SemaphoreType.DMA((LOADS,))]
        work = 2 * fields.size
    return pl.pallas_call(
        body,
        in_specs=[SMEM] * len(scalars) + specs,
        out_specs=jax.tree.map(lambda _: VMEM, out_shape),
        out_shape=out_shape,
        scratch_shapes=scratch,
        compiler_params=LIMIT if fields is None else ALL,
        cost_estimate=pl.CostEstimate(
            flops=4 * work, bytes_accessed=6 * work, transcendentals=0
        ),
        name=name,
    )(*scalars, *arrays)


def finish_kernel(halves_ref, *refs, chunks, width):
    *pieces, across, down, out_across, out_down = refs
    for (turn, contents), piece in zip(chunks, pieces):
        lanes = pl.ds(pl.multiple_of(halves_ref[turn] * width, width), width)
        at = 0
        for kind, first, rows in contents:
            conduct, out = (down, out_down) if kind == "down" else (across, out_across)
            out[first : first + rows, lanes] = (
                conduct[first : first + rows, lanes] * piece[at : at + rows]
            )
            at += rows


def finish(chunks, halves, pieces, conduct_across, conduct_down):
    shape = jax.ShapeDtypeStruct(conduct_across.shape, jnp.float32)
    return pl.pallas_call(
        functools.partial(finish_kernel, chunks=chunks, width=pieces[0].shape[1]),
        in_specs=[SMEM] + [VMEM] * (len(pieces) + 2),
        out_specs=[VMEM, VMEM],
        out_shape=[shape, shape],
        compiler_params=LIMIT,
        name="finish",
    )(halves, *pieces, conduct_across, conduct_down)


def after(value, *others):
    return lax.optimization_barrier((value, *others))[0]


def towards(index, step, size):
    return index ^ step if size & (size - 1) == 0 else (index + step) % size


def source(index, step, size):
    return index ^ step if size & (size - 1) == 0 else (index + size - step) % size


def local(potentials, pair_include, labels, conduct_across, conduct_down):
    parts, strips = lax.axis_size("cores"), lax.axis_size("strip")
    core, strip = lax.axis_index("cores"), lax.axis_index("strip")
    each, height, width = potentials.shape
    rows = labels.shape[0]
    turns = strips // parts

    flat = [(c, s // turns, s % turns) for c in range(parts) for s in range(strips)]

    def number(c, group, j):
        return c * strips + group * turns + j

    def move(array, to):
        moves = [(number(*at), number(*to(*at))) for at in flat]
        return lax.ppermute(array, ("cores", "strip"), moves)

    def send_home(array, turn):
        return move(
            array, lambda c, g, j: (g, towards(c, g, parts), towards(j, turn, turns))
        )

    def exchange(block, k):
        moves = [(i, towards(i, k, parts)) for i in range(parts)]
        return lax.ppermute(block, "cores", moves)

    inside = strip % turns
    ts = jnp.arange(turns, dtype=jnp.int32)
    ks = jnp.arange(parts, dtype=jnp.int32)
    base = source(core, ks, parts) * each
    region = towards(towards(core, ks, parts), strip // turns, parts)
    first = region[:, None] * turns + towards(inside, ts, turns)[None]
    last = (strip == strips - 1).astype(jnp.int32)
    first = jnp.concatenate([first.reshape(-1), last[None]])
    halves = source(inside, ts, turns)

    block = jax.ShapeDtypeStruct((turns, each, rows, width), jnp.bfloat16)
    column = jax.ShapeDtypeStruct((height, LANES), jnp.float32)
    *down, edge = on_tile(
        down_kernel, "down", [block] * parts + [column], [first], fields=potentials
    )
    far = list(range(parts - 1, 0, -1))
    beside = lax.ppermute(edge, "strip", [(i, i - 1) for i in range(1, strips)])
    labels = move(labels, lambda c, g, j: (source(g, c, parts), c, j))
    down = after(tuple(down), labels)
    down = [down[0], *[exchange(down[k], k) for k in far][::-1]]
    groups, linear = prepare(after(pair_include, edge))

    own_labels = []
    for t in range(turns):
        to = towards(inside, t, turns)
        part = lax.dynamic_slice_in_dim(labels, to * width, width, 1)
        back = (turns - t) % turns if turns & (turns - 1) else t
        own_labels.append((back, move(part, lambda c, g, j: (c, g, towards(j, t, turns))) if t else part))
    own_labels = [part for _, part in sorted(own_labels, key=lambda pair: pair[0])]

    block = jax.ShapeDtypeStruct((1, each, rows, width), jnp.bfloat16)
    side = on_tile(
        functools.partial(side_kernel, turns=turns),
        "side",
        [block] * (parts * turns),
        [after(first, *own_labels, groups)],
        potentials,
        beside,
    )
    factors = on_tile(
        factors_kernel,
        "factors",
        jax.ShapeDtypeStruct((turns, parts * each, rows, width), jnp.bfloat16),
        [],
        jnp.concatenate(own_labels, axis=0),
        after(linear, *side),
    )
    blocks = [side[t * parts : (t + 1) * parts] for t in range(turns)]
    def band_sums(t, got):
        return pairs(base, groups, got, own_labels[t], factors, t, t)

    down[0] = after(down[0], *down[1:])
    down_sums = [band_sums(0, down)]
    arrived = []
    for t in range(turns):
        got = [blocks[t][0]]
        for k in far:
            waits = [factors] if t == 0 else down_sums[-1:]
            got.insert(1, exchange(after(blocks[t][k], *waits), k))
        arrived.append(got)
    down[0] = after(down[0], arrived[0][1])
    down_sums += [band_sums(t, down) for t in range(1, turns)]
    side_sums, pieces = [], []
    for t in range(turns):
        got = arrived[t]
        got[0] = after(got[0], (side_sums or down_sums)[-1])
        side_sums.append(pairs(base, groups, got, own_labels[t], factors, 0, t))
        joined = jnp.concatenate([down_sums[t], side_sums[t]], axis=0)
        pieces.append(send_home(joined, t))
    contents = tuple((t, (("down", 0, rows), ("side", 0, rows))) for t in range(turns))
    return finish(contents, halves, pieces, conduct_across, conduct_down)


def solution(mesh):
    return jax.shard_map(
        local,
        mesh=mesh,
        in_specs=(
            P("cores", None, "strip"),
            P(),
            P("strip", "cores"),
            P("strip", "cores"),
            P("strip", "cores"),
        ),
        out_specs=(P("strip", "cores"), P("strip", "cores")),
        check_vma=False,
    )
```

```python
import functools

import jax
import jax.numpy as jnp
from jax import lax
from jax.experimental import pallas as pl
from jax.experimental.pallas import tpu as pltpu
from jax.sharding import PartitionSpec as P

PARTNERS = 4
LOW = -64.0
LANES = 128
VMEM = pl.BlockSpec(memory_space=pltpu.VMEM)
SMEM = pl.BlockSpec(memory_space=pltpu.SMEM)
HBM = pl.BlockSpec(memory_space=pltpu.HBM)
LOADS = 4
LIMIT = pltpu.CompilerParams(vmem_limit_bytes=16 * 2**20)
ALL = pltpu.CompilerParams(vmem_limit_bytes=60 * 2**20)


def prepare_kernel(include_ref, groups_ref, linear_ref):
    fields = include_ref.shape[0]
    slots = groups_ref.shape[1]
    f32 = jnp.float32

    def dot(a, b, over):
        return lax.dot_general(
            a.astype(jnp.bfloat16),
            b.astype(jnp.bfloat16),
            ((over[:1], over[1:]), ((), ())),
            preferred_element_type=f32,
        )

    row = lax.broadcasted_iota(jnp.int32, (fields, fields), 0)
    column = lax.broadcasted_iota(jnp.int32, (fields, fields), 1)
    upper = jnp.where(column > row, 1.0, 0.0)
    lower = jnp.where(column < row, 1.0, 0.0)
    eye = jnp.where(column == row, 1.0, 0.0)
    included = jnp.where(column > row, include_ref[...], 0).astype(f32)
    both = included + dot(included, eye, (0, 0))
    many = jnp.sum(jnp.sum(included, axis=1, keepdims=True), axis=0, keepdims=True)
    rest = jnp.where(many > fields * (fields - 1) / 4, 1.0, 0.0)
    listed = jnp.where(rest > 0, upper - included, included)
    place = dot(listed, upper, (1, 0))
    count = jnp.sum(listed, axis=1, keepdims=True)
    degree = jnp.sum(both, axis=1, keepdims=True)
    groups = jnp.floor((count + (PARTNERS - 1)) * (1.0 / PARTNERS))
    start = dot(lower, jnp.broadcast_to(groups, (fields, LANES)), (1, 0))[:, :1]
    total = jnp.sum(groups, axis=0, keepdims=True)
    slot = lax.broadcasted_iota(jnp.int32, (fields, slots), 1).astype(f32)
    ids = lax.broadcasted_iota(jnp.int32, (fields, slots), 0).astype(f32)
    inside = jnp.where((slot >= start) & (slot < start + groups), 1.0, 0.0)
    used = jnp.sum(inside, axis=0, keepdims=True)
    own = jnp.sum(inside * ids, axis=0, keepdims=True)
    first = jnp.sum(inside * (slot - start) * PARTNERS, axis=0, keepdims=True)
    places = dot(jnp.where(listed > 0, place, -8.0), inside, (0, 0))
    places = jnp.where(used > 0, places, -8.0)
    groups_ref[...] = jnp.zeros(groups_ref.shape, jnp.int32)
    for u in range(PARTNERS):
        hit = jnp.where(places == first + u, 1.0, 0.0)
        found = jnp.sum(hit, axis=0, keepdims=True)
        partner = jnp.sum(hit * ids, axis=0, keepdims=True)
        absent = jnp.where(used > 0, float(fields), float(fields + 1))
        groups_ref[u : u + 1, :] = jnp.where(found > 0, partner, absent).astype(jnp.int32)
    owner = jnp.where(used > 0, own, float(fields + 1))
    groups_ref[PARTNERS : PARTNERS + 1, :] = owner.astype(jnp.int32)
    groups_ref[PARTNERS + 1 : PARTNERS + 2, :] = jnp.broadcast_to(total, (1, slots)).astype(
        jnp.int32
    )
    groups_ref[PARTNERS + 2 : PARTNERS + 3, :] = jnp.broadcast_to(rest, (1, slots)).astype(
        jnp.int32
    )
    lanes = linear_ref.shape[1]
    padding = (2.0 - 4.0 * rest) * (groups * PARTNERS - count)
    wide = jnp.concatenate([both, jnp.zeros((fields, lanes - fields), f32)], axis=1)
    row = lax.broadcasted_iota(jnp.int32, (fields, lanes), 0)
    column = lax.broadcasted_iota(jnp.int32, (fields, lanes), 1)
    linear_ref[...] = jnp.where(row == column, 0.0, degree + wide) + padding


def prepare(pair_include):
    fields = pair_include.shape[0]
    most = sum(pl.cdiv(fields - 1 - a, PARTNERS) for a in range(fields))
    slots = pl.cdiv(most + 8, LANES) * LANES
    groups, linear = pl.pallas_call(
        prepare_kernel,
        out_shape=(
            jax.ShapeDtypeStruct((8, slots), jnp.int32),
            jax.ShapeDtypeStruct((fields, LANES), jnp.float32),
        ),
        compiler_params=LIMIT,
        name="prepare",
    )(pair_include)
    return groups.T.reshape(-1), linear


def factors_kernel(labels_ref, linear_ref, out_ref):
    turns, fields, band, width = out_ref.shape

    def one(field, carry):
        table = jnp.broadcast_to(linear_ref[pl.ds(field, 1), :], (band, LANES))
        for t in range(turns):
            mine = labels_ref[t * band : (t + 1) * band, :]
            factor = jnp.concatenate(
                [
                    jnp.take_along_axis(table, mine[:, at : at + LANES], axis=1)
                    for at in range(0, width, LANES)
                ],
                axis=1,
            )
            out_ref[t, field] = factor.astype(jnp.bfloat16)
        return carry

    lax.fori_loop(0, fields, one, 0, unroll=4)


def sort_steps(size):
    p = 1
    while p < size:
        k = p
        while k >= 1:
            for j in range(k % p, size - k, 2 * k):
                for i in range(min(k, size - j - k)):
                    if (i + j) // (2 * p) == (i + j + k) // (2 * p):
                        yield i + j, i + j + k
            k //= 2
        p *= 2


def compare(values, steps):
    for i, j in steps:
        low = jnp.minimum(values[i], values[j])
        values[j] = jnp.maximum(values[i], values[j])
        values[i] = low
    return values


def merge_steps(size):
    k = size // 2
    while k >= 1:
        for i in range(size):
            if not i & k:
                yield i, i + k
        k //= 2


def rank_sums(held, ranked, out_ref):
    fields = ranked.shape[0]
    rows, width = out_ref.shape
    half = fields // 2
    columns = width // LANES

    def block(number, carry):
        place = (
            pl.ds(pl.multiple_of(number // columns * 8, 8), 8),
            pl.ds(pl.multiple_of(number % columns * LANES, LANES), LANES),
        )
        for start in (0, half):
            values = [held[(start + i, *place)] for i in range(half)]
            for i, value in enumerate(compare(values, sort_steps(half))):
                ranked[start + i] = value
        total = jnp.zeros((8, LANES), jnp.float32)
        for start, pick in ((0, jnp.minimum), (half, jnp.maximum)):
            values = [
                pick(ranked[i], ranked[fields - 1 - i]) for i in range(half)
            ]
            for i, value in enumerate(compare(values, merge_steps(half))):
                if start + i:
                    total = total + value * float(start + i)
        out_ref[place] = total
        return carry

    lax.fori_loop(0, rows // 8 * columns, block, 0)


def pairs_kernel(base_ref, groups_ref, *refs, scale, unroll, at_turn, label_turn):
    *parts, labels_ref, factors_ref, out_ref, held, ranked = refs
    fields = factors_ref.shape[1]
    _, each, rows, width = parts[0].shape
    held[fields] = jnp.full((rows, width), LOW, jnp.float32)
    held[fields + 1] = jnp.zeros((rows, width), jnp.float32)
    labels = labels_ref[...]
    linear = jnp.zeros((rows, width), jnp.float32)
    for k, part in enumerate(parts):
        for i in range(each):
            field = base_ref[k] + i
            values = jnp.where(labels == field, LOW, part[at_turn, i].astype(jnp.float32))
            held[field] = values
            linear = linear + factors_ref[label_turn, field].astype(jnp.float32) * values

    out_ref[...] = jnp.zeros((rows, width), jnp.float32)

    @pl.when(groups_ref[PARTNERS + 2] == 1)
    def _():
        rank_sums(held, ranked, out_ref)

    def step(number, total):
        for v in range(unroll):
            at = (number * unroll + v) * 8
            own = held[groups_ref[at + PARTNERS]]
            for u in range(PARTNERS):
                total = total + jnp.maximum(own, held[groups_ref[at + u]])
        return total

    steps = (groups_ref[PARTNERS + 1] + (unroll - 1)) // unroll
    total = lax.fori_loop(0, steps, step, jnp.zeros((rows, width), jnp.float32))
    sign = 1.0 - 2.0 * groups_ref[PARTNERS + 2].astype(jnp.float32)
    out_ref[...] = (2.0 * (out_ref[...] + sign * total) - linear) * scale


def pairs(base, groups, parts, labels, factors, at_turn, label_turn):
    fields = factors.shape[1]
    work = fields * fields * labels.size
    return pl.pallas_call(
        functools.partial(
            pairs_kernel,
            scale=2.0 / (fields * (fields - 1)),
            unroll=8,
            at_turn=at_turn,
            label_turn=label_turn,
        ),
        in_specs=[SMEM, SMEM] + [VMEM] * (len(parts) + 2),
        out_specs=VMEM,
        out_shape=jax.ShapeDtypeStruct(labels.shape, jnp.float32),
        scratch_shapes=[
            pltpu.VMEM((fields + 2, *labels.shape), jnp.float32),
            pltpu.VMEM((fields, 8, LANES), jnp.float32),
        ],
        compiler_params=LIMIT,
        cost_estimate=pl.CostEstimate(flops=work, bytes_accessed=work // 16, transcendentals=0),
        name="pairs",
    )(base, groups, *parts, labels, factors)


def load_fields(potentials_ref, held, sems):
    each = held.shape[0]
    step = max(each // LOADS, 1)
    copies = []
    for number, at in enumerate(range(0, each, step)):
        span = pl.ds(at, step)
        copies.append(
            pltpu.make_async_copy(potentials_ref.at[span], held.at[span], sems.at[number])
        )
        copies[-1].start()
    for number, copy in enumerate(copies):
        copy.wait()
        yield from range(number * step, (number + 1) * step)


def down_kernel(potentials_ref, *refs):
    *outs, edge_ref, held, sems = refs
    parts = len(outs)
    core, strip = lax.axis_index("cores"), lax.axis_index("strip")
    _, height, width = held.shape
    turns, _, rows, _ = outs[0].shape
    row = lax.broadcasted_iota(jnp.int32, (rows, width), 0)
    lane = lax.broadcasted_iota(jnp.int32, (height, LANES), 1)
    for i in load_fields(potentials_ref, held, sems):
        for k, out in enumerate(outs):
            for t in range(turns):
                region = towards(towards(core, k, parts), lax.div(strip, turns), parts)
                band = region * turns + towards(lax.rem(strip, turns), t, turns)
                first = pl.multiple_of(band * rows, rows)
                following = pl.multiple_of(jnp.minimum(first + rows, height - 8), 8)
                at_end = first + rows == height
                here = held[i, pl.ds(first, rows), :]
                below = held[i, pl.ds(following, 8), :]
                below = jnp.concatenate([here[1:], below[:1]], axis=0)
                change = jnp.where((row == rows - 1) & at_end, 0.0, below - here)
                out[t, i] = change.astype(jnp.bfloat16)
        edge_ref[...] = jnp.where(lane == i, held[i, :, 0:1], edge_ref[...] if i else 0.0)


def side_kernel(first_ref, potentials_ref, beside_ref, *outs, turns):
    _, each, rows, width = outs[0].shape
    parts = len(outs) // turns
    lane = lax.broadcasted_iota(jnp.int32, (rows, width), 1)
    at_end = first_ref[len(outs)] == 1
    for k in range(parts):
        for t in range(turns):
            first = pl.multiple_of(first_ref[k * turns + t] * rows, rows)
            for i in range(each):
                here = potentials_ref[i, pl.ds(first, rows), :]
                right = pltpu.roll(here, width - 1, 1)
                beside = beside_ref[pl.ds(first, rows), i : i + 1]
                right = jnp.where(lane == width - 1, beside, right)
                change = jnp.where((lane == width - 1) & at_end, 0.0, right - here)
                outs[t * parts + k][0, i] = change.astype(jnp.bfloat16)


def on_tile(body, name, out_shape, scalars, *arrays, fields=None):
    work = sum(a.size for a in arrays)
    specs = [VMEM] * len(arrays)
    scratch = []
    if fields is not None:
        arrays, specs = (fields, *arrays), [HBM, *specs]
        scratch = [pltpu.VMEM(fields.shape, fields.dtype), pltpu.SemaphoreType.DMA((LOADS,))]
        work = 2 * fields.size
    return pl.pallas_call(
        body,
        in_specs=[SMEM] * len(scalars) + specs,
        out_specs=jax.tree.map(lambda _: VMEM, out_shape),
        out_shape=out_shape,
        scratch_shapes=scratch,
        compiler_params=LIMIT if fields is None else ALL,
        cost_estimate=pl.CostEstimate(
            flops=4 * work, bytes_accessed=6 * work, transcendentals=0
        ),
        name=name,
    )(*scalars, *arrays)


def finish_kernel(halves_ref, *refs, chunks, width):
    *pieces, across, down, out_across, out_down = refs
    for (turn, contents), piece in zip(chunks, pieces):
        lanes = pl.ds(pl.multiple_of(halves_ref[turn] * width, width), width)
        at = 0
        for kind, first, rows in contents:
            conduct, out = (down, out_down) if kind == "down" else (across, out_across)
            out[first : first + rows, lanes] = (
                conduct[first : first + rows, lanes] * piece[at : at + rows]
            )
            at += rows


def finish(chunks, halves, pieces, conduct_across, conduct_down):
    shape = jax.ShapeDtypeStruct(conduct_across.shape, jnp.float32)
    return pl.pallas_call(
        functools.partial(finish_kernel, chunks=chunks, width=pieces[0].shape[1]),
        in_specs=[SMEM] + [VMEM] * (len(pieces) + 2),
        out_specs=[VMEM, VMEM],
        out_shape=[shape, shape],
        compiler_params=LIMIT,
        name="finish",
    )(halves, *pieces, conduct_across, conduct_down)


def after(value, *others):
    return lax.optimization_barrier((value, *others))[0]


def towards(index, step, size):
    return index ^ step if size & (size - 1) == 0 else (index + step) % size


def source(index, step, size):
    return index ^ step if size & (size - 1) == 0 else (index + size - step) % size


def local(potentials, pair_include, labels, conduct_across, conduct_down):
    parts, strips = lax.axis_size("cores"), lax.axis_size("strip")
    core, strip = lax.axis_index("cores"), lax.axis_index("strip")
    each, height, width = potentials.shape
    rows = labels.shape[0]
    turns = strips // parts

    flat = [(c, s // turns, s % turns) for c in range(parts) for s in range(strips)]

    def number(c, group, j):
        return c * strips + group * turns + j

    def move(array, to):
        moves = [(number(*at), number(*to(*at))) for at in flat]
        return lax.ppermute(array, ("cores", "strip"), moves)

    def send_home(array, turn):
        return move(
            array, lambda c, g, j: (g, towards(c, g, parts), towards(j, turn, turns))
        )

    def exchange(block, k):
        moves = [(i, towards(i, k, parts)) for i in range(parts)]
        return lax.ppermute(block, "cores", moves)

    inside = strip % turns
    ts = jnp.arange(turns, dtype=jnp.int32)
    ks = jnp.arange(parts, dtype=jnp.int32)
    base = source(core, ks, parts) * each
    region = towards(towards(core, ks, parts), strip // turns, parts)
    first = region[:, None] * turns + towards(inside, ts, turns)[None]
    last = (strip == strips - 1).astype(jnp.int32)
    first = jnp.concatenate([first.reshape(-1), last[None]])
    halves = source(inside, ts, turns)

    block = jax.ShapeDtypeStruct((turns, each, rows, width), jnp.bfloat16)
    column = jax.ShapeDtypeStruct((height, LANES), jnp.float32)
    *down, edge = on_tile(
        down_kernel, "down", [block] * parts + [column], [], fields=potentials
    )
    far = list(range(parts - 1, 0, -1))
    labels = move(labels, lambda c, g, j: (source(g, c, parts), c, j))
    edge = after(edge, labels)
    beside = lax.ppermute(edge, "strip", [(i, i - 1) for i in range(1, strips)])
    down = after(tuple(down), labels)
    down = [down[0], *[exchange(down[k], k) for k in far][::-1]]
    groups, linear = prepare(after(pair_include, edge))

    own_labels = []
    for t in range(turns):
        to = towards(inside, t, turns)
        part = lax.dynamic_slice_in_dim(labels, to * width, width, 1)
        back = (turns - t) % turns if turns & (turns - 1) else t
        own_labels.append((back, move(part, lambda c, g, j: (c, g, towards(j, t, turns))) if t else part))
    own_labels = [part for _, part in sorted(own_labels, key=lambda pair: pair[0])]

    block = jax.ShapeDtypeStruct((1, each, rows, width), jnp.bfloat16)
    side = on_tile(
        functools.partial(side_kernel, turns=turns),
        "side",
        [block] * (parts * turns),
        [after(first, *own_labels, groups)],
        potentials,
        beside,
    )
    factors = on_tile(
        factors_kernel,
        "factors",
        jax.ShapeDtypeStruct((turns, parts * each, rows, width), jnp.bfloat16),
        [],
        jnp.concatenate(own_labels, axis=0),
        after(linear, *side),
    )
    blocks = [side[t * parts : (t + 1) * parts] for t in range(turns)]
    def band_sums(t, got):
        return pairs(base, groups, got, own_labels[t], factors, t, t)

    down[0] = after(down[0], *down[1:])
    down_sums = [band_sums(0, down)]
    arrived = []
    for t in range(turns):
        got = [blocks[t][0]]
        for k in far:
            waits = [factors] if t == 0 else down_sums[-1:]
            got.insert(1, exchange(after(blocks[t][k], *waits), k))
        arrived.append(got)
    down[0] = after(down[0], arrived[0][1])
    down_sums += [band_sums(t, down) for t in range(1, turns)]
    side_sums, pieces = [], []
    for t in range(turns):
        got = arrived[t]
        got[0] = after(got[0], (side_sums or down_sums)[-1])
        side_sums.append(pairs(base, groups, got, own_labels[t], factors, 0, t))
        joined = jnp.concatenate([down_sums[t], side_sums[t]], axis=0)
        pieces.append(send_home(joined, t))
    contents = tuple((t, (("down", 0, rows), ("side", 0, rows))) for t in range(turns))
    return finish(contents, halves, pieces, conduct_across, conduct_down)


def solution(mesh):
    return jax.shard_map(
        local,
        mesh=mesh,
        in_specs=(
            P("cores", None, "strip"),
            P(),
            P("strip", "cores"),
            P("strip", "cores"),
            P("strip", "cores"),
        ),
        out_specs=(P("strip", "cores"), P("strip", "cores")),
        check_vma=False,
    )
```

```python
import functools

import jax
import jax.numpy as jnp
from jax import lax
from jax.experimental import pallas as pl
from jax.experimental.pallas import tpu as pltpu
from jax.sharding import PartitionSpec as P

PARTNERS = 4
LOW = -64.0
LANES = 128
VMEM = pl.BlockSpec(memory_space=pltpu.VMEM)
SMEM = pl.BlockSpec(memory_space=pltpu.SMEM)
HBM = pl.BlockSpec(memory_space=pltpu.HBM)
LOADS = 4
LIMIT = pltpu.CompilerParams(vmem_limit_bytes=16 * 2**20)
ALL = pltpu.CompilerParams(vmem_limit_bytes=60 * 2**20)


def prepare_kernel(include_ref, groups_ref, linear_ref):
    fields = include_ref.shape[0]
    slots = groups_ref.shape[1]
    f32 = jnp.float32

    def dot(a, b, over):
        return lax.dot_general(
            a.astype(jnp.bfloat16),
            b.astype(jnp.bfloat16),
            ((over[:1], over[1:]), ((), ())),
            preferred_element_type=f32,
        )

    row = lax.broadcasted_iota(jnp.int32, (fields, fields), 0)
    column = lax.broadcasted_iota(jnp.int32, (fields, fields), 1)
    upper = jnp.where(column > row, 1.0, 0.0)
    lower = jnp.where(column < row, 1.0, 0.0)
    eye = jnp.where(column == row, 1.0, 0.0)
    included = jnp.where(column > row, include_ref[...], 0).astype(f32)
    both = included + dot(included, eye, (0, 0))
    many = jnp.sum(jnp.sum(included, axis=1, keepdims=True), axis=0, keepdims=True)
    rest = jnp.where(many > fields * (fields - 1) / 4, 1.0, 0.0)
    listed = jnp.where(rest > 0, upper - included, included)
    place = dot(listed, upper, (1, 0))
    count = jnp.sum(listed, axis=1, keepdims=True)
    degree = jnp.sum(both, axis=1, keepdims=True)
    groups = jnp.floor((count + (PARTNERS - 1)) * (1.0 / PARTNERS))
    start = dot(lower, jnp.broadcast_to(groups, (fields, LANES)), (1, 0))[:, :1]
    total = jnp.sum(groups, axis=0, keepdims=True)
    slot = lax.broadcasted_iota(jnp.int32, (fields, slots), 1).astype(f32)
    ids = lax.broadcasted_iota(jnp.int32, (fields, slots), 0).astype(f32)
    inside = jnp.where((slot >= start) & (slot < start + groups), 1.0, 0.0)
    used = jnp.sum(inside, axis=0, keepdims=True)
    own = jnp.sum(inside * ids, axis=0, keepdims=True)
    first = jnp.sum(inside * (slot - start) * PARTNERS, axis=0, keepdims=True)
    places = dot(jnp.where(listed > 0, place, -8.0), inside, (0, 0))
    places = jnp.where(used > 0, places, -8.0)
    groups_ref[...] = jnp.zeros(groups_ref.shape, jnp.int32)
    for u in range(PARTNERS):
        hit = jnp.where(places == first + u, 1.0, 0.0)
        found = jnp.sum(hit, axis=0, keepdims=True)
        partner = jnp.sum(hit * ids, axis=0, keepdims=True)
        absent = jnp.where(used > 0, float(fields), float(fields + 1))
        groups_ref[u : u + 1, :] = jnp.where(found > 0, partner, absent).astype(jnp.int32)
    owner = jnp.where(used > 0, own, float(fields + 1))
    groups_ref[PARTNERS : PARTNERS + 1, :] = owner.astype(jnp.int32)
    groups_ref[PARTNERS + 1 : PARTNERS + 2, :] = jnp.broadcast_to(total, (1, slots)).astype(
        jnp.int32
    )
    groups_ref[PARTNERS + 2 : PARTNERS + 3, :] = jnp.broadcast_to(rest, (1, slots)).astype(
        jnp.int32
    )
    lanes = linear_ref.shape[1]
    padding = (2.0 - 4.0 * rest) * (groups * PARTNERS - count)
    wide = jnp.concatenate([both, jnp.zeros((fields, lanes - fields), f32)], axis=1)
    row = lax.broadcasted_iota(jnp.int32, (fields, lanes), 0)
    column = lax.broadcasted_iota(jnp.int32, (fields, lanes), 1)
    linear_ref[...] = jnp.where(row == column, 0.0, degree + wide) + padding


def prepare(pair_include):
    fields = pair_include.shape[0]
    most = sum(pl.cdiv(fields - 1 - a, PARTNERS) for a in range(fields))
    slots = pl.cdiv(most + 8, LANES) * LANES
    groups, linear = pl.pallas_call(
        prepare_kernel,
        out_shape=(
            jax.ShapeDtypeStruct((8, slots), jnp.int32),
            jax.ShapeDtypeStruct((fields, LANES), jnp.float32),
        ),
        compiler_params=LIMIT,
        name="prepare",
    )(pair_include)
    return groups.T.reshape(-1), linear


def factors_kernel(labels_ref, linear_ref, out_ref):
    turns, fields, band, width = out_ref.shape

    def one(field, carry):
        table = jnp.broadcast_to(linear_ref[pl.ds(field, 1), :], (band, LANES))
        for t in range(turns):
            mine = labels_ref[t * band : (t + 1) * band, :]
            factor = jnp.concatenate(
                [
                    jnp.take_along_axis(table, mine[:, at : at + LANES], axis=1)
                    for at in range(0, width, LANES)
                ],
                axis=1,
            )
            out_ref[t, field] = factor.astype(jnp.bfloat16)
        return carry

    lax.fori_loop(0, fields, one, 0, unroll=4)


def sort_steps(size):
    p = 1
    while p < size:
        k = p
        while k >= 1:
            for j in range(k % p, size - k, 2 * k):
                for i in range(min(k, size - j - k)):
                    if (i + j) // (2 * p) == (i + j + k) // (2 * p):
                        yield i + j, i + j + k
            k //= 2
        p *= 2


def compare(values, steps):
    for i, j in steps:
        low = jnp.minimum(values[i], values[j])
        values[j] = jnp.maximum(values[i], values[j])
        values[i] = low
    return values


def merge_steps(size):
    k = size // 2
    while k >= 1:
        for i in range(size):
            if not i & k:
                yield i, i + k
        k //= 2


def rank_sums(held, ranked, out_ref):
    fields = ranked.shape[0]
    rows, width = out_ref.shape
    half = fields // 2
    columns = width // LANES

    def block(number, carry):
        place = (
            pl.ds(pl.multiple_of(number // columns * 8, 8), 8),
            pl.ds(pl.multiple_of(number % columns * LANES, LANES), LANES),
        )
        for start in (0, half):
            values = [held[(start + i, *place)] for i in range(half)]
            for i, value in enumerate(compare(values, sort_steps(half))):
                ranked[start + i] = value
        total = jnp.zeros((8, LANES), jnp.float32)
        for start, pick in ((0, jnp.minimum), (half, jnp.maximum)):
            values = [
                pick(ranked[i], ranked[fields - 1 - i]) for i in range(half)
            ]
            for i, value in enumerate(compare(values, merge_steps(half))):
                if start + i:
                    total = total + value * float(start + i)
        out_ref[place] = total
        return carry

    lax.fori_loop(0, rows // 8 * columns, block, 0)


def pairs_kernel(base_ref, groups_ref, *refs, scale, unroll, at_turn, label_turn):
    *parts, labels_ref, factors_ref, out_ref, held, ranked = refs
    fields = factors_ref.shape[1]
    _, each, rows, width = parts[0].shape
    held[fields] = jnp.full((rows, width), LOW, jnp.float32)
    held[fields + 1] = jnp.zeros((rows, width), jnp.float32)
    labels = labels_ref[...]
    linear = jnp.zeros((rows, width), jnp.float32)
    for k, part in enumerate(parts):
        for i in range(each):
            field = base_ref[k] + i
            values = jnp.where(labels == field, LOW, part[at_turn, i].astype(jnp.float32))
            held[field] = values
            linear = linear + factors_ref[label_turn, field].astype(jnp.float32) * values

    out_ref[...] = jnp.zeros((rows, width), jnp.float32)

    @pl.when(groups_ref[PARTNERS + 2] == 1)
    def _():
        rank_sums(held, ranked, out_ref)

    def step(number, total):
        for v in range(unroll):
            at = (number * unroll + v) * 8
            own = held[groups_ref[at + PARTNERS]]
            for u in range(PARTNERS):
                total = total + jnp.maximum(own, held[groups_ref[at + u]])
        return total

    steps = (groups_ref[PARTNERS + 1] + (unroll - 1)) // unroll
    total = lax.fori_loop(0, steps, step, jnp.zeros((rows, width), jnp.float32))
    sign = 1.0 - 2.0 * groups_ref[PARTNERS + 2].astype(jnp.float32)
    out_ref[...] = (2.0 * (out_ref[...] + sign * total) - linear) * scale


def pairs(base, groups, parts, labels, factors, at_turn, label_turn):
    fields = factors.shape[1]
    work = fields * fields * labels.size
    return pl.pallas_call(
        functools.partial(
            pairs_kernel,
            scale=2.0 / (fields * (fields - 1)),
            unroll=8,
            at_turn=at_turn,
            label_turn=label_turn,
        ),
        in_specs=[SMEM, SMEM] + [VMEM] * (len(parts) + 2),
        out_specs=VMEM,
        out_shape=jax.ShapeDtypeStruct(labels.shape, jnp.float32),
        scratch_shapes=[
            pltpu.VMEM((fields + 2, *labels.shape), jnp.float32),
            pltpu.VMEM((fields, 8, LANES), jnp.float32),
        ],
        compiler_params=LIMIT,
        cost_estimate=pl.CostEstimate(flops=work, bytes_accessed=work // 16, transcendentals=0),
        name="pairs",
    )(base, groups, *parts, labels, factors)


def down_of(potentials_ref, place, first, row, base, height):
    rows = row.shape[0]
    following = jnp.minimum(first + rows, height - 8)
    here = potentials_ref[(*place, pl.ds(pl.multiple_of(first - base, 8), rows))]
    below = potentials_ref[(*place, pl.ds(pl.multiple_of(following - base, 8), 8))]
    below = jnp.concatenate([here[1:], below[:1]], axis=0)
    at_end = first + rows == height
    return jnp.where((row == rows - 1) & at_end, 0.0, below - here).astype(jnp.bfloat16)


def edge_kernel(potentials_ref, out_ref):
    each, rows, _ = potentials_ref.shape
    lane = lax.broadcasted_iota(jnp.int32, (rows, LANES), 1)
    edge = jnp.zeros((rows, LANES), jnp.float32)
    for i in range(each):
        edge = jnp.where(lane == i, potentials_ref[i, :, 0:1], edge)
    out_ref[...] = edge


def down_kernel(potentials_ref, *refs):
    *outs, held, sems = refs
    parts = len(outs) + 1
    core, strip = lax.axis_index("cores"), lax.axis_index("strip")
    _, each, span, width = held.shape
    height = potentials_ref.shape[1]
    turns, _, rows, _ = outs[0].shape
    row = lax.broadcasted_iota(jnp.int32, (rows, width), 0)
    step = max(each // LOADS, 1)
    regions, bases = [], []
    for k in range(len(outs)):
        region = towards(towards(core, k + 1, parts), lax.div(strip, turns), parts)
        regions.append(region)
        bases.append(pl.multiple_of(jnp.minimum(region * (turns * rows), height - span), 8))

    def load(number, k):
        some = pl.ds(number * step, step)
        return pltpu.make_async_copy(
            potentials_ref.at[some, pl.ds(bases[k], span)], held.at[k, some], sems.at[number, k]
        )

    for number in range(each // step):
        for k in range(len(outs)):
            load(number, k).start()
    for number in range(each // step):
        for k, out in enumerate(outs):
            load(number, k).wait()
            for t in range(turns):
                band = regions[k] * turns + towards(lax.rem(strip, turns), t, turns)
                first = band * rows
                for i in range(number * step, (number + 1) * step):
                    out[t, i] = down_of(held, (k, i), first, row, bases[k], height)


def side_kernel(first_ref, potentials_ref, beside_ref, own_down, *outs, turns):
    _, each, rows, width = outs[0].shape
    parts = len(outs) // turns
    lane = lax.broadcasted_iota(jnp.int32, (rows, width), 1)
    row = lax.broadcasted_iota(jnp.int32, (rows, width), 0)
    for t in range(turns):
        first = pl.multiple_of(first_ref[t] * rows, rows)
        for i in range(each):
            own_down[t, i] = down_of(potentials_ref, (i,), first, row, 0, potentials_ref.shape[1])
    at_end = first_ref[len(outs)] == 1
    for k in range(parts):
        for t in range(turns):
            first = pl.multiple_of(first_ref[k * turns + t] * rows, rows)
            for i in range(each):
                here = potentials_ref[i, pl.ds(first, rows), :]
                right = pltpu.roll(here, width - 1, 1)
                beside = beside_ref[pl.ds(first, rows), i : i + 1]
                right = jnp.where(lane == width - 1, beside, right)
                change = jnp.where((lane == width - 1) & at_end, 0.0, right - here)
                outs[t * parts + k][0, i] = change.astype(jnp.bfloat16)


def on_tile(body, name, out_shape, scalars, *arrays, fields=None):
    work = sum(a.size for a in arrays)
    specs = [VMEM] * len(arrays)
    scratch = []
    if fields is not None:
        arrays, specs = (fields, *arrays), [HBM, *specs]
        turns, each, rows, width = out_shape[0].shape
        held = (len(out_shape), each, turns * rows + 8, width)
        scratch = [
            pltpu.VMEM(held, fields.dtype),
            pltpu.SemaphoreType.DMA((LOADS, len(out_shape))),
        ]
        work = 2 * fields.size
    return pl.pallas_call(
        body,
        in_specs=[SMEM] * len(scalars) + specs,
        out_specs=jax.tree.map(lambda _: VMEM, out_shape),
        out_shape=out_shape,
        scratch_shapes=scratch,
        compiler_params=LIMIT if fields is None else ALL,
        cost_estimate=pl.CostEstimate(
            flops=4 * work, bytes_accessed=6 * work, transcendentals=0
        ),
        name=name,
    )(*scalars, *arrays)


def finish_kernel(halves_ref, *refs, chunks, width):
    *pieces, across, down, out_across, out_down = refs
    for (turn, contents), piece in zip(chunks, pieces):
        lanes = pl.ds(pl.multiple_of(halves_ref[turn] * width, width), width)
        at = 0
        for kind, first, rows in contents:
            conduct, out = (down, out_down) if kind == "down" else (across, out_across)
            out[first : first + rows, lanes] = (
                conduct[first : first + rows, lanes] * piece[at : at + rows]
            )
            at += rows


def finish(chunks, halves, pieces, conduct_across, conduct_down):
    shape = jax.ShapeDtypeStruct(conduct_across.shape, jnp.float32)
    return pl.pallas_call(
        functools.partial(finish_kernel, chunks=chunks, width=pieces[0].shape[1]),
        in_specs=[SMEM] + [VMEM] * (len(pieces) + 2),
        out_specs=[VMEM, VMEM],
        out_shape=[shape, shape],
        compiler_params=LIMIT,
        name="finish",
    )(halves, *pieces, conduct_across, conduct_down)


def after(value, *others):
    return lax.optimization_barrier((value, *others))[0]


def towards(index, step, size):
    return index ^ step if size & (size - 1) == 0 else (index + step) % size


def source(index, step, size):
    return index ^ step if size & (size - 1) == 0 else (index + size - step) % size


def local(potentials, pair_include, labels, conduct_across, conduct_down):
    parts, strips = lax.axis_size("cores"), lax.axis_size("strip")
    core, strip = lax.axis_index("cores"), lax.axis_index("strip")
    each, height, width = potentials.shape
    rows = labels.shape[0]
    turns = strips // parts

    flat = [(c, s // turns, s % turns) for c in range(parts) for s in range(strips)]

    def number(c, group, j):
        return c * strips + group * turns + j

    def move(array, to):
        moves = [(number(*at), number(*to(*at))) for at in flat]
        return lax.ppermute(array, ("cores", "strip"), moves)

    def send_home(array, turn):
        return move(
            array, lambda c, g, j: (g, towards(c, g, parts), towards(j, turn, turns))
        )

    def exchange(block, k):
        moves = [(i, towards(i, k, parts)) for i in range(parts)]
        return lax.ppermute(block, "cores", moves)

    inside = strip % turns
    ts = jnp.arange(turns, dtype=jnp.int32)
    ks = jnp.arange(parts, dtype=jnp.int32)
    base = source(core, ks, parts) * each
    region = towards(towards(core, ks, parts), strip // turns, parts)
    first = region[:, None] * turns + towards(inside, ts, turns)[None]
    last = (strip == strips - 1).astype(jnp.int32)
    first = jnp.concatenate([first.reshape(-1), last[None]])
    halves = source(inside, ts, turns)

    block = jax.ShapeDtypeStruct((turns, each, rows, width), jnp.bfloat16)
    column = jax.ShapeDtypeStruct((height, LANES), jnp.float32)
    sent = on_tile(down_kernel, "down", [block] * (parts - 1), [], fields=potentials)
    far = list(range(parts - 1, 0, -1))
    labels = move(labels, lambda c, g, j: (source(g, c, parts), c, j))
    edge = on_tile(edge_kernel, "edge", column, [], after(potentials, *sent, labels))
    beside = lax.ppermute(edge, "strip", [(i, i - 1) for i in range(1, strips)])
    sent = after(tuple(sent), labels)
    sent = [exchange(sent[k - 1], k) for k in far][::-1]
    groups, linear = prepare(after(pair_include, edge))

    own_labels = []
    for t in range(turns):
        to = towards(inside, t, turns)
        part = lax.dynamic_slice_in_dim(labels, to * width, width, 1)
        back = (turns - t) % turns if turns & (turns - 1) else t
        own_labels.append((back, move(part, lambda c, g, j: (c, g, towards(j, t, turns))) if t else part))
    own_labels = [part for _, part in sorted(own_labels, key=lambda pair: pair[0])]

    one = jax.ShapeDtypeStruct((1, each, rows, width), jnp.bfloat16)
    own_down, *side = on_tile(
        functools.partial(side_kernel, turns=turns),
        "side",
        [block] + [one] * (parts * turns),
        [after(first, *own_labels, groups)],
        potentials,
        beside,
    )
    factors = on_tile(
        factors_kernel,
        "factors",
        jax.ShapeDtypeStruct((turns, parts * each, rows, width), jnp.bfloat16),
        [],
        jnp.concatenate(own_labels, axis=0),
        after(linear, *side),
    )
    blocks = [side[t * parts : (t + 1) * parts] for t in range(turns)]
    def band_sums(t, got):
        return pairs(base, groups, got, own_labels[t], factors, t, t)

    down = [after(own_down, *sent), *sent]
    down_sums = [band_sums(0, down)]
    arrived = []
    for t in range(turns):
        got = [blocks[t][0]]
        for k in far:
            waits = [factors] if t == 0 else down_sums[-1:]
            got.insert(1, exchange(after(blocks[t][k], *waits), k))
        arrived.append(got)
    down[0] = after(down[0], arrived[0][1])
    down_sums += [band_sums(t, down) for t in range(1, turns)]
    side_sums, pieces = [], []
    for t in range(turns):
        got = arrived[t]
        got[0] = after(got[0], (side_sums or down_sums)[-1])
        side_sums.append(pairs(base, groups, got, own_labels[t], factors, 0, t))
        joined = jnp.concatenate([down_sums[t], side_sums[t]], axis=0)
        pieces.append(send_home(joined, t))
    contents = tuple((t, (("down", 0, rows), ("side", 0, rows))) for t in range(turns))
    return finish(contents, halves, pieces, conduct_across, conduct_down)


def solution(mesh):
    return jax.shard_map(
        local,
        mesh=mesh,
        in_specs=(
            P("cores", None, "strip"),
            P(),
            P("strip", "cores"),
            P("strip", "cores"),
            P("strip", "cores"),
        ),
        out_specs=(P("strip", "cores"), P("strip", "cores")),
        check_vma=False,
    )
```
